32 devices in a mesh: wide: 4 (over z), narrow: 8 (over y, x, core).
Axes of the slice: x: 2, y: 2, z: 4, core: 2. Of those that a mesh axis runs over, the one named last changes fastest.
Arguments:
- frames: bfloat16 [16384, 2048], P('narrow', 'wide'), may hold values from -6 to 6
- weights: bfloat16 [2, 2048, 2048], P(None, 'narrow', 'wide'), may hold values from -0.125 to 0.125
- gains: float32 [2, 2048], P(None, 'wide'), may hold values from 0.1 to 1.9
- shifts: float32 [2, 2048], P(None, 'wide'), may hold values from -3 to 3
- decays: float32 [2, 2048], P(None, 'wide'), may hold values from 0.3 to 0.97
- resets: int32 [16384], P('narrow'), may hold values 0 or 1
- running: float32 [2, 2, 2048], P(None, None, 'wide'), may hold values from 0.5 to 2
- grad_out: bfloat16 [16384, 2048], P('narrow', 'wide'), may hold values from -6 to 6
Outputs:
- activations: bfloat16 [16384, 2048], P('narrow', 'wide')
- input_grad: float32 [16384, 2048], P('narrow', 'wide')
- weight_grad: float32 [2, 2048, 2048], P(None, 'narrow', 'wide')
- gain_grad: float32 [2, 2048], P(None, 'wide')
- shift_grad: float32 [2, 2048], P(None, 'wide')
- decay_grad: float32 [2, 2048], P(None, 'wide')
- running_new: float32 [2, 2, 2048], P(None, None, 'wide')
The draws below stay inside these ranges and needn't reach their ends.
All inputs are finite; a program needn't handle non-finite values. No bound on the sum of `resets` on one device may be relied on, other than what follows from the above.
Results may differ from the reference program's by a relative error of at most 0.0047.
Values may be sent and summed in bfloat16 or wider, within the bound.
No kernel may reach another device: no remote copies, remote signals or barrier semaphores. Data moves between devices by JAX's collectives and lax.ppermute only.
A program may use at most 192 MiB of HBM per device.

```python
import jax
import jax.numpy as jnp
from jax import lax

D = 2048
LENGTH = 1024
FRAMES = 16384


def set_ends(array, own_key, low, largest):
    dims = array.shape
    spot = [jax.random.randint(jax.random.fold_in(own_key, axis), (), 0, dims[axis]) for axis in range(len(dims))]
    array = array.at[tuple(spot)].set(low)
    longest = dims.index(max(dims))
    spot[longest] = (spot[longest] + 1) % dims[longest]
    return array.at[tuple(spot)].set(largest)


def shard_levels(rng, extent, cuts, low, largest):
    level, own = 1.0, jax.random.fold_in(rng, 6)
    for dim, blocks in cuts:
        steps = jnp.exp(jax.random.uniform(jax.random.fold_in(own, dim), (blocks,), jnp.float32, low / len(cuts), largest / len(cuts)))
        level = level * jnp.repeat(steps, extent[dim] // blocks).reshape([-1 if axis == dim else 1 for axis in range(len(extent))])
    return level


def bell_draw(stream_key, dims, spread, limit, pieces=(), kind=jnp.bfloat16):
    result = jax.random.normal(stream_key, dims, jnp.float32) * spread
    if len(pieces) > 0:
        result = shard_levels(stream_key, dims, pieces, -0.22, 0.18) * result
    return jnp.clip(result, min=-limit, max=limit).astype(kind)


def setup_inputs(seed: int = 0) -> dict:
    key_list = jax.random.split(jax.random.key(seed), 9)
    frames = bell_draw(key_list[0], (FRAMES, D), 1.0, 6.0, ((0, 8), (1, 4)))
    weights = bell_draw(key_list[1], (2, D, D), D ** -0.5, 0.125, ((1, 8), (2, 4)))
    gains = jnp.clip(1.0 + 0.18 * jax.random.normal(key_list[2], (2, D), jnp.float32), 0.1, 1.9)
    shifts = bell_draw(key_list[3], (2, D), 0.2, 3.0, ((1, 4),), jnp.float32)
    decays = jnp.clip(0.3 + 0.67 * jax.random.uniform(key_list[4], (2, D), jnp.float32) ** shard_levels(key_list[4], (2, D), ((1, 4),), -0.2, 0.2), 0.3, 0.97)
    resets = set_ends((jax.random.randint(key_list[5], (FRAMES,), 0, 64) < 1).astype(jnp.int32), jax.random.fold_in(key_list[5], 1), 0, 1)
    running = jnp.clip(0.5 + 1.5 * jax.random.uniform(key_list[6], (2, 2, D), jnp.float32) ** shard_levels(key_list[6], (2, 2, D), ((2, 4),), -0.2, 0.2), 0.5, 2.0)
    grad_out = bell_draw(key_list[7], (FRAMES, D), 1.0, 6.0, ((0, 8), (1, 4)))
    return {"frames": frames, "weights": weights, "gains": gains, "shifts": shifts, "decays": decays, "resets": resets, "running": running, "grad_out": grad_out}


@jax.custom_vjp
def low(v):
    return lax.optimization_barrier(v.astype(jnp.bfloat16)).astype(jnp.float32)

@jax.custom_vjp
def low_back(v):
    return v

def low_keep(v):
    return (low(v), None)

def low_pass(kept, grad):
    return (grad,)

def back_keep(v):
    return (v, None)

def back_low(kept, grad):
    return (low(grad),)
low.defvjp(low_keep, low_pass)
low_back.defvjp(back_keep, back_low)
eps_norm = 1e-05
momentum = 0.1

def recur_step(state, inputs):
    rate, drive = inputs
    state = rate * state + drive
    return (state, state)

def layer(inputs, weight, gain, shift, decay, keep):
    pre = low_back(jnp.dot(inputs, weight, precision=lax.Precision.HIGHEST))
    mean = lax.optimization_barrier(jnp.mean(pre, axis=0))
    var = lax.optimization_barrier(jnp.mean(pre * pre, axis=0)) - mean * mean
    normed = (pre - mean) * lax.rsqrt(var + eps_norm) * gain + shift
    drive = normed.reshape(-1, LENGTH, D).transpose(1, 0, 2)
    rate = keep.reshape(-1, LENGTH).transpose(1, 0)[:, :, None] * decay
    start = jnp.zeros((drive.shape[1], D), jnp.float32)
    _, states = lax.scan(jax.checkpoint(recur_step), start, (rate, drive))
    states = states.transpose(1, 0, 2).reshape(-1, D)
    return (low(jax.nn.silu(states)), (mean, var))

def reference(frames, weights, gains, shifts, decays, resets, running, grad_out):
    keep = (1 - resets).astype(jnp.float32)

    def forward(inputs, weight_all, gain_all, shift_all, decay_all):
        stats = []
        for level in range(2):
            inputs, stat = layer(inputs, weight_all[level], gain_all[level], shift_all[level], decay_all[level], keep)
            stats.append(stat)
        return (inputs, stats)
    output, pull, stats = jax.vjp(forward, frames.astype(jnp.float32), weights.astype(jnp.float32), gains, shifts, decays, has_aux=True)
    grads = pull(grad_out.astype(jnp.float32))
    count = FRAMES * 1.0
    updated = []
    for level in range(2):
        new_mean = (1.0 - momentum) * running[level, 0] + momentum * stats[level][0]
        new_var = (1.0 - momentum) * running[level, 1] + momentum * stats[level][1] * count / (count - 1.0)
        updated.append(jnp.stack([new_mean, new_var]))
    running_new = jnp.stack(updated)
    return (output.astype(jnp.bfloat16), grads[0], grads[1], grads[2], grads[3], grads[4], running_new)
```

```python
import functools

import jax
import jax.numpy as jnp
from jax import lax
from jax.experimental import pallas as pl
from jax.experimental.pallas import tpu as pltpu
from jax.sharding import PartitionSpec as P

LENGTH = 1024


eps_norm = 1e-05
momentum = 0.1

f32 = jnp.float32
bf16 = jnp.bfloat16
BIG = 56 * 2**20
AXES = ("wide", "narrow")


def whole(space=pltpu.VMEM):
    return pl.BlockSpec(memory_space=space)


def stats_of(sums, count):
    mean = sums[0] / count
    var = sums[1] / count - mean * mean
    return mean, var, lax.rsqrt(var + eps_norm)


def product_kernel(xs, xo, ws, wo, pre, sums):
    acc = jnp.dot(xs[...], ws[...], preferred_element_type=f32)
    acc = acc + jnp.dot(xo[...], wo[...], preferred_element_type=f32)
    parts = acc.shape[1] // 128
    for g in range(acc.shape[0] // 8):
        for k in range(parts):
            pre[pl.ds(g * 8 * parts + k, 8, stride=parts), :] = acc[g * 8 : g * 8 + 8, k * 128 : k * 128 + 128]

    @pl.when(pl.program_id(0) == 0)
    def _():
        sums[...] = jnp.zeros_like(sums)

    sums[0:1, :] += jnp.sum(acc, 0, keepdims=True)
    sums[1:2, :] += jnp.sum(acc * acc, 0, keepdims=True)


def product(xs, xo, ws, wo, step=256):
    rows, depth = xs.shape
    cols = ws.shape[1]
    parts = cols // 128
    pre, sums = pl.pallas_call(
        product_kernel,
        grid=(rows // step,),
        in_specs=[
            pl.BlockSpec((step, depth), lambda i: (i, 0)),
            pl.BlockSpec((step, depth), lambda i: (i, 0)),
            pl.BlockSpec((depth, cols), lambda i: (0, 0)),
            pl.BlockSpec((depth, cols), lambda i: (0, 0)),
        ],
        out_specs=[
            pl.BlockSpec((step * parts, 128), lambda i: (i, 0)),
            pl.BlockSpec((2, cols), lambda i: (0, 0)),
        ],
        out_shape=[
            jax.ShapeDtypeStruct((rows * parts, 128), f32),
            jax.ShapeDtypeStruct((2, cols), f32),
        ],
        compiler_params=pltpu.CompilerParams(vmem_limit_bytes=BIG),
        cost_estimate=pl.CostEstimate(flops=4 * rows * depth * cols, bytes_accessed=12 << 20, transcendentals=0),
    )(xs, xo, ws, wo)
    return pre, sums.reshape(2, parts, 128)


def forward_kernel(count, sums, params, keep, pre, states, y):
    mean, _, rstd = stats_of(sums, count)
    sc = params[0] * rstd
    sh = params[1] - mean * sc
    decay = params[2]
    parts = sc.shape[0]
    rows = y.shape[0]

    def step(i, h):
        for u in range(8):
            t = i * 8 + u
            at = pl.ds(pl.multiple_of(t * parts, parts), parts)
            h = (decay * keep[t]) * h + (pre[at, :] * sc + sh)
            states[at, :] = h
        return h

    lax.fori_loop(0, rows // 8, step, jnp.zeros_like(sc))

    def turn(g, _):
        for k in range(parts):
            two = []
            for u in range(2):
                h = states[pl.ds((g * 2 + u) * 8 * parts + k, 8, stride=parts), :]
                two.append(h / (1.0 + jnp.exp(-h)))
            y[pl.ds(pl.multiple_of(g * 16, 16), 16), k * 128 : k * 128 + 128] = jnp.concatenate(two, 0).astype(bf16)
        return 0

    lax.fori_loop(0, rows // 16, turn, 0)


def forward(sums, params, keep, pre, count):
    parts = params.shape[1]
    rows = pre.shape[0] // parts
    return pl.pallas_call(
        functools.partial(forward_kernel, count),
        in_specs=[whole(), whole(), whole(pltpu.SMEM), whole()],
        out_specs=[whole(), whole()],
        out_shape=[
            jax.ShapeDtypeStruct(pre.shape, f32),
            jax.ShapeDtypeStruct((rows, parts * 128), bf16),
        ],
        compiler_params=pltpu.CompilerParams(vmem_limit_bytes=BIG),
        cost_estimate=pl.CostEstimate(flops=12 * pre.size, bytes_accessed=10 * pre.size, transcendentals=pre.size),
    )(sums, params, keep, pre)


def backward_kernel(count, n_dy, sums, params, keep, pre, states, *rest):
    dys, (carried, totals, dyt) = rest[:n_dy], rest[n_dy:]
    mean, _, rstd = stats_of(sums, count)
    shift = -mean * rstd
    decay = params[2]
    parts = decay.shape[0]
    rows = dys[0].shape[0]

    def turn(g, _):
        at = pl.ds(pl.multiple_of(g * 16, 16), 16)
        for k in range(parts):
            v = dys[0][at, k * 128 : k * 128 + 128].astype(f32)
            for d in dys[1:]:
                v = v + d[at, k * 128 : k * 128 + 128].astype(f32)
            for u in range(2):
                dyt[pl.ds((g * 2 + u) * 8 * parts + k, 8, stride=parts), :] = v[u * 8 : u * 8 + 8]
        return 0

    lax.fori_loop(0, rows // 16, turn, 0)

    def one(t, h, prior, carry):
        back, sg, sx, sd = carry
        at = pl.ds(pl.multiple_of(t * parts, parts), parts)
        s = 1.0 / (1.0 + jnp.exp(-h))
        g = dyt[at, :] * (s + h * s * (1.0 - s)) + back
        carried[at, :] = g
        gk = g * keep[t]
        return (gk * decay, sg + g, sx + g * (pre[at, :] * rstd + shift), sd + gk * prior)

    def get(t):
        return states[pl.ds(pl.multiple_of(t * parts, parts), parts), :]

    def step(i, carry):
        for u in range(8):
            t = rows - 1 - (i * 8 + u)
            carry = one(t, get(t), get(t - 1), carry)
        return carry

    zero = jnp.zeros_like(decay)
    carry = lax.fori_loop(0, rows // 8 - 1, step, (zero, zero, zero, zero))
    for t in range(7, -1, -1):
        carry = one(t, get(t), get(t - 1) if t else zero, carry)
    totals[0], totals[1], totals[2] = carry[1], carry[2], carry[3]


def backward(sums, params, keep, pre, states, dys, count):
    parts = params.shape[1]
    return pl.pallas_call(
        functools.partial(backward_kernel, count, len(dys)),
        in_specs=[whole(), whole(), whole(pltpu.SMEM), whole(), whole()] + [whole()] * len(dys),
        out_specs=[whole(), whole()],
        out_shape=[
            jax.ShapeDtypeStruct(pre.shape, f32),
            jax.ShapeDtypeStruct((3, parts, 128), f32),
        ],
        scratch_shapes=[pltpu.VMEM(pre.shape, f32)],
        compiler_params=pltpu.CompilerParams(vmem_limit_bytes=BIG),
        cost_estimate=pl.CostEstimate(flops=24 * pre.size, bytes_accessed=16 * pre.size, transcendentals=pre.size),
    )(sums, params, keep, pre, states, *dys)


def spread_kernel(count, sums, params, totals, carried, pre, ws, wo, dpre, same, other):
    mean, _, rstd = stats_of(sums, count)
    sc = params[0] * rstd
    slope = sc * rstd * (totals[1] / count)
    c3 = mean * slope - sc * (totals[0] / count)
    parts = sc.shape[0]
    for g in range(dpre.shape[0] // 16):
        for k in range(parts):
            two = []
            for u in range(2):
                at = pl.ds((g * 2 + u) * 8 * parts + k, 8, stride=parts)
                two.append(sc[k : k + 1] * carried[at, :] - slope[k : k + 1] * pre[at, :] + c3[k : k + 1])
            dpre[g * 16 : g * 16 + 16, k * 128 : k * 128 + 128] = jnp.concatenate(two, 0).astype(bf16)
    d = dpre[...]
    dims = (((1,), (1,)), ((), ()))
    same[...] = lax.dot_general(d, ws[...], dims, preferred_element_type=f32)
    other[...] = lax.dot_general(d, wo[...], dims, preferred_element_type=f32).astype(bf16)


def spread(sums, params, totals, carried, pre, ws, wo, count, step=256):
    parts = params.shape[1]
    rows, cols = pre.shape[0] // parts, parts * 128
    depth = ws.shape[0]
    small = pl.BlockSpec((None, parts, 128), lambda i: (0, 0, 0))
    return pl.pallas_call(
        functools.partial(spread_kernel, count),
        grid=(rows // step,),
        in_specs=[
            pl.BlockSpec(sums.shape, lambda i: (0, 0, 0)),
            pl.BlockSpec(params.shape, lambda i: (0, 0, 0)),
            pl.BlockSpec(totals.shape, lambda i: (0, 0, 0)),
            pl.BlockSpec((step * parts, 128), lambda i: (i, 0)),
            pl.BlockSpec((step * parts, 128), lambda i: (i, 0)),
            pl.BlockSpec((depth, cols), lambda i: (0, 0)),
            pl.BlockSpec((depth, cols), lambda i: (0, 0)),
        ],
        out_specs=[
            pl.BlockSpec((step, cols), lambda i: (i, 0)),
            pl.BlockSpec((step, depth), lambda i: (i, 0)),
            pl.BlockSpec((step, depth), lambda i: (i, 0)),
        ],
        out_shape=[
            jax.ShapeDtypeStruct((rows, cols), bf16),
            jax.ShapeDtypeStruct((rows, depth), f32),
            jax.ShapeDtypeStruct((rows, depth), bf16),
        ],
        compiler_params=pltpu.CompilerParams(vmem_limit_bytes=BIG),
        cost_estimate=pl.CostEstimate(flops=4 * rows * depth * cols, bytes_accessed=20 << 20, transcendentals=0),
    )(sums, params, totals, carried, pre, ws, wo)


def paired(frames, weights, gains, shifts, decays, resets, running, grad_out):
    wide, narrow = lax.axis_size("wide"), lax.axis_size("narrow")
    rows, lanes = frames.shape
    half = lanes // 2
    depth = weights.shape[1]
    count = rows * narrow * 1.0
    z = lax.axis_index("wide")
    n = lax.axis_index("narrow")
    r, c = n // 2, n % 2
    slot = 2 * (z % 2) + c

    def send(x, to):
        pairs = []
        for a in range(wide):
            for b in range(narrow):
                tz, tr, tc = to(a, b // 2, b % 2)
                pairs.append((a * narrow + b, tz * narrow + tr * 2 + tc))
        return lax.ppermute(x, AXES, pairs)

    def swap(x):
        return send(x, lambda a, b, d: (a, b, 1 - d))

    def over_ring(x, m):
        return send(x, lambda a, b, d: (a, b ^ m, d))

    def over_wide(x, m):
        return send(x, lambda a, b, d: (a ^ m, b, d))

    def everywhere(x):
        a1, a2, a3 = over_ring(x, 1), over_ring(x, 2), over_ring(x, 3)
        x = (x + a1) + (a2 + a3)
        a1, a2, a3 = over_wide(x, 1), over_wide(x, 2), over_wide(x, 3)
        return (x + a1) + (a2 + a3)

    def placed(pieces, shape, spots):
        buf = jnp.zeros(shape, pieces[0].dtype)
        for piece, spot in zip(pieces, spots, strict=True):
            buf = lax.dynamic_update_slice(buf, piece, spot)
        return buf

    def to_rows(x):
        got = []
        for m in range(wide):
            q = z ^ m
            piece = lax.dynamic_slice(x, ((q // 2) * LENGTH, (q % 2) * half), (LENGTH, half))
            got.append(send(piece, lambda a, b, d: (2 * d + ((a ^ m) >> 1), b, (a ^ m) & 1)))
        return got

    def from_rows(x):
        got = []
        for m in range(wide):
            piece = lax.dynamic_slice(x, (0, (slot ^ m) * half), (LENGTH, half))
            got.append(send(piece, lambda a, b, d: ((2 * (a & 1) + d) ^ m, b, a >> 1)))
        return got

    def by_slot(pieces, s):
        return placed(pieces, (LENGTH, wide * half), [(0, (s ^ m) * half) for m in range(wide)])

    def home(pieces):
        spots = [(((z ^ m) // 2) * LENGTH, ((z ^ m) % 2) * half) for m in range(wide)]
        return placed(pieces, (rows, lanes), spots)

    def gathered(w):
        own = lax.dynamic_slice(w, (0, c * half), (depth, half))
        away = swap(lax.dynamic_slice(w, (0, (1 - c) * half), (depth, half)))
        both = jnp.stack([own, away])
        pieces = [both] + [over_wide(both, m) for m in range(1, wide)]
        line = placed(pieces, (2, depth, wide * half), [(0, 0, (z ^ m) * half) for m in range(wide)])
        result = []
        for part, (first, second) in ((line[0], (1, 2)), (line[1], (2, 1))):
            p1 = over_ring(part, first)
            p2 = over_ring(part, second)
            p3 = over_ring(p1, second)
            spots = [((r ^ m) * depth, 0) for m in (0, first, second, 3)]
            result.append(placed([part, p1, p2, p3], (4 * depth, wide * half), spots))
        return result

    def scattered(parts):
        done = []
        for part, (first, second) in ((parts[0], (1, 2)), (parts[1], (2, 1))):

            def block(m, part=part):
                return lax.dynamic_slice(part, ((r ^ m) * depth, 0), (depth, wide * half))

            g3 = over_ring(block(3).astype(bf16), first)
            g1 = over_ring(block(first).astype(bf16), first)
            mid = (block(second) + g3.astype(f32)).astype(bf16)
            g2 = over_ring(mid, second)
            done.append(block(0) + g1.astype(f32) + g2.astype(f32))
        line = jnp.stack(done)

        def col(m):
            return lax.dynamic_slice(line, (0, 0, (z ^ m) * half), (2, depth, half))

        got = [over_wide(col(m).astype(bf16), m).astype(f32) for m in range(1, wide)]
        total = (col(0) + got[0]) + (got[1] + got[2])
        own, away = total[0], swap(total[1])
        return jnp.concatenate([jnp.where(c == 0, own, away), jnp.where(c == 0, away, own)], axis=1)

    theirs = swap(resets)
    row = jnp.where(c == z // 2, resets, theirs)
    keep = 1.0 - lax.dynamic_slice(row, ((z % 2) * LENGTH,), (LENGTH,)).astype(f32)
    vectors = jnp.concatenate([gains, shifts, decays])
    vectors = lax.dynamic_slice(vectors, (0, c * half), (6, half))
    pieces = [vectors] + [over_wide(vectors, m) for m in range(1, wide)]
    vectors = placed(pieces, (6, wide * half), [(0, (z ^ m) * half) for m in range(wide)])
    vectors = vectors.reshape(3, 2, -1, 128)
    params = [vectors[:, level] for level in range(2)]

    mats = [gathered(weights[0])]
    got = to_rows(frames)
    xs = by_slot(got, slot)
    xo = by_slot([swap(p) for p in got], slot ^ 1)
    mats.append(gathered(weights[1]))
    grads = by_slot(to_rows(grad_out), slot)

    saved = []
    ins = (xs, xo)
    for level in range(2):
        pre, sums = product(*ins, *mats[level])
        sums = everywhere(sums)
        states, y = forward(sums, params[level], keep, pre, count)
        saved.append((ins, pre, sums, states))
        if level == 0:
            ins = (y, swap(y))
    sent = from_rows(y)

    dys = (grads,)
    weight_list = [None, None]
    totals_list = [None, None]
    for level in (1, 0):
        ins, pre, sums, states = saved[level]
        carried, totals = backward(sums, params[level], keep, pre, states, dys, count)
        totals = everywhere(totals)
        totals_list[level] = totals
        dpre, same, other = spread(sums, params[level], totals, carried, pre, *mats[level], count)
        other = swap(other)
        dys = (same, other)
        if level == 0:
            back = from_rows((same + other.astype(f32)).astype(bf16))
        dims = (((0,), (0,)), ((), ()))
        weight_list[level] = scattered(
            [lax.dot_general(x, dpre, dims, preferred_element_type=f32) for x in ins]
        )

    small = []
    for level in range(2):
        mean, var, _ = stats_of(saved[level][2], count)
        small.append(jnp.concatenate([mean[None], var[None], totals_list[level]]))
    small = jnp.stack(small).reshape(2, 5, wide, half)
    small = lax.dynamic_index_in_dim(small, z, 2, keepdims=False)
    away = swap(small)
    small = jnp.concatenate([jnp.where(c == 0, small, away), jnp.where(c == 0, away, small)], axis=2)
    new_mean = (1.0 - momentum) * running[:, 0] + momentum * small[:, 0]
    new_var = (1.0 - momentum) * running[:, 1] + momentum * small[:, 1] * count / (count - 1.0)
    return (
        home(sent),
        home(back).astype(f32),
        jnp.stack(weight_list),
        small[:, 3],
        small[:, 2],
        small[:, 4],
        jnp.stack([new_mean, new_var], axis=1),
    )


def link(earlier, later):
    return (earlier[0] * later[0], later[0] * earlier[1] + later[1])


def general(frames, weights, gains, shifts, decays, resets, running, grad_out):
    frame_rows, lanes = frames.shape
    count = frame_rows * lax.axis_size("narrow") * 1.0
    keep = (1 - resets).astype(jnp.float32).reshape(-1, LENGTH, 1)
    layer_in = frames
    saved = []
    updated = []
    for level in range(2):
        full_in = lax.all_gather(layer_in, "wide", axis=1, tiled=True)
        full_weight = lax.all_gather(weights[level], "narrow", axis=0, tiled=True)
        pre = jnp.dot(full_in, full_weight, preferred_element_type=jnp.float32)
        total, squares = lax.psum((jnp.sum(pre, 0), jnp.sum(pre * pre, 0)), "narrow")
        mean = total / count
        var = squares / count - mean * mean
        scale = lax.rsqrt(var + eps_norm)
        normed_hat = (pre - mean) * scale
        drive = (normed_hat * gains[level] + shifts[level]).reshape(-1, LENGTH, lanes)
        rate = keep * decays[level]
        _, states = lax.associative_scan(link, (rate, drive), axis=1)
        saved.append((full_in, full_weight, normed_hat, scale, states, rate))
        states = states.reshape(frame_rows, lanes)
        layer_in = jax.nn.silu(states).astype(jnp.bfloat16)
        new_mean = (1.0 - momentum) * running[level, 0] + momentum * mean
        new_var = (1.0 - momentum) * running[level, 1] + momentum * var * count / (count - 1.0)
        updated.append(jnp.stack([new_mean, new_var]))
    grad = grad_out.astype(jnp.float32)
    weight_list = [None, None]
    gain_list = [None, None]
    shift_list = [None, None]
    decay_list = [None, None]
    for level in (1, 0):
        full_in, full_weight, normed_hat, scale, states, rate = saved[level]
        sigma = jax.nn.sigmoid(states)
        grad_state = grad.reshape(-1, LENGTH, lanes) * (sigma + states * sigma * (1.0 - sigma))
        rate_next = jnp.concatenate([rate[:, 1:], jnp.zeros_like(rate[:, :1])], axis=1)
        _, carried = lax.associative_scan(link, (rate_next, grad_state), reverse=True, axis=1)
        prior = jnp.concatenate([jnp.zeros_like(states[:, :1]), states[:, :-1]], axis=1)
        decay_term = jnp.sum(carried * keep * prior, axis=(0, 1))
        carried = carried.reshape(frame_rows, lanes)
        shift_sum, gain_sum, decay_sum = lax.psum(
            (jnp.sum(carried, 0), jnp.sum(carried * normed_hat, 0), decay_term), "narrow"
        )
        grad_pre = (
            gains[level] * scale * (carried - shift_sum / count - normed_hat * gain_sum / count)
        ).astype(jnp.bfloat16)
        weight_list[level] = lax.psum_scatter(
            lax.dot_general(
                full_in, grad_pre, (((0,), (0,)), ((), ())), preferred_element_type=jnp.float32
            ),
            "narrow",
            scatter_dimension=0,
            tiled=True,
        )
        gain_list[level] = gain_sum
        shift_list[level] = shift_sum
        decay_list[level] = decay_sum
        partial_term = lax.dot_general(
            grad_pre, full_weight, (((1,), (1,)), ((), ())), preferred_element_type=jnp.float32
        )
        grad = lax.psum_scatter(partial_term, "wide", scatter_dimension=1, tiled=True)
    return (
        layer_in,
        grad,
        jnp.stack(weight_list),
        jnp.stack(gain_list),
        jnp.stack(shift_list),
        jnp.stack(decay_list),
        jnp.stack(updated),
    )


def per_device(frames, weights, *rest):
    wide, narrow = lax.axis_size("wide"), lax.axis_size("narrow")
    rows, lanes = frames.shape
    one_row_a_chip = 2 * rows == wide * LENGTH and wide == 4 and narrow == 2 * wide
    if one_row_a_chip and lanes == 2 * weights.shape[1] and wide * lanes == 2048:
        return paired(frames, weights, *rest)
    return general(frames, weights, *rest)


def solution(mesh):
    placed = (
        P("narrow", "wide"),
        P(None, "narrow", "wide"),
        P(None, "wide"),
        P(None, "wide"),
        P(None, "wide"),
        P("narrow"),
        P(None, None, "wide"),
        P("narrow", "wide"),
    )
    return jax.shard_map(
        per_device,
        mesh=mesh,
        in_specs=placed,
        out_specs=(
            P("narrow", "wide"),
            P("narrow", "wide"),
            P(None, "narrow", "wide"),
            P(None, "wide"),
            P(None, "wide"),
            P(None, "wide"),
            P(None, None, "wide"),
        ),
        check_vma=False,
    )
```

```python
import functools

import jax
import jax.numpy as jnp
from jax import lax
from jax.experimental import pallas as pl
from jax.experimental.pallas import tpu as pltpu
from jax.sharding import Mesh
from jax.sharding import PartitionSpec as P

LENGTH = 1024


eps_norm = 1e-05
momentum = 0.1

f32 = jnp.float32
bf16 = jnp.bfloat16
BIG = 56 * 2**20
AXES = ("wide", "ring", "core")
NARROW = ("ring", "core")


def whole(space=pltpu.VMEM):
    return pl.BlockSpec(memory_space=space)


def stats_of(sums, count):
    mean = sums[0] / count
    var = sums[1] / count - mean * mean
    return mean, var, lax.rsqrt(var + eps_norm)


def tile_of(w, r, z, side, by_row):
    return w[r, z, side] if by_row else w[z, r, side]


def product_kernel(by_row, xs, xo, w, pre, sums):
    blocks, rows, width = xs.shape
    per = width // 128
    parts = blocks * per

    @pl.when(pl.program_id(0) == 0)
    def _():
        sums[...] = jnp.zeros_like(sums)

    for z in range(blocks):
        acc = None
        for side, x in enumerate((xs, xo)):
            for r in range(blocks):
                term = jnp.dot(x[r], tile_of(w, r, z, side, by_row), preferred_element_type=f32)
                acc = term if acc is None else acc + term
        for k in range(per):
            piece = acc[:, k * 128 : k * 128 + 128]
            at = z * per + k
            for g in range(rows // 8):
                pre[pl.ds(g * 8 * parts + at, 8, stride=parts), :] = piece[g * 8 : g * 8 + 8]
            sums[0, at : at + 1, :] += jnp.sum(piece, 0, keepdims=True)
            sums[1, at : at + 1, :] += jnp.sum(piece * piece, 0, keepdims=True)


def product(xs, xo, w, by_row, step=256):
    blocks, rows, width = xs.shape
    cols = blocks * width
    parts = cols // 128
    return pl.pallas_call(
        functools.partial(product_kernel, by_row),
        grid=(rows // step,),
        in_specs=[
            pl.BlockSpec((blocks, step, width), lambda i: (0, i, 0)),
            pl.BlockSpec((blocks, step, width), lambda i: (0, i, 0)),
            pl.BlockSpec(w.shape, lambda i: (0, 0, 0, 0, 0)),
        ],
        out_specs=[
            pl.BlockSpec((step * parts, 128), lambda i: (i, 0)),
            pl.BlockSpec((2, parts, 128), lambda i: (0, 0, 0)),
        ],
        out_shape=[
            jax.ShapeDtypeStruct((rows * parts, 128), f32),
            jax.ShapeDtypeStruct((2, parts, 128), f32),
        ],
        compiler_params=pltpu.CompilerParams(vmem_limit_bytes=BIG),
        cost_estimate=pl.CostEstimate(flops=4 * rows * cols * cols, bytes_accessed=12 << 20, transcendentals=0),
    )(xs, xo, w)


def forward_kernel(count, sums, params, keep, pre, states, *rest):
    ys, held = rest[:-1], rest[-1]
    mean, _, rstd = stats_of(sums, count)
    sc = params[0] * rstd
    sh = params[1] - mean * sc
    decay = params[2]
    parts = sc.shape[0]
    rows, width = ys[0].shape[1:]
    per = width // 128
    groups = rows // 16
    block, blocks = pl.program_id(0), pl.num_programs(0)
    first = block * rows

    @pl.when(block == 0)
    def _():
        held[...] = jnp.zeros_like(held)

    def scan(g, h):
        for u in range(16):
            t = g * 16 + u
            at = pl.ds(pl.multiple_of(t * parts, parts), parts)
            h = (decay * keep[first + t]) * h + (pre[at, :] * sc + sh)
            states[at, :] = h
        return h

    def turn(y, g):
        for k in range(parts):
            two = []
            for u in range(2):
                h = states[pl.ds((g * 16 + u * 8) * parts + k, 8, stride=parts), :]
                two.append(h / (1.0 + jnp.exp(-h)))
            lane = k % per * 128
            at = pl.ds(pl.multiple_of(g * 16, 16), 16)
            y[k // per, at, lane : lane + 128] = jnp.concatenate(two, 0).astype(bf16)

    def run(y):
        def both(g, h):
            turn(y, g - 1)
            return scan(g, h)

        held[...] = lax.fori_loop(1, groups, both, scan(0, held[...]))
        turn(y, groups - 1)

    for n, y in enumerate(ys):
        pl.when(block // (blocks // len(ys)) == n)(functools.partial(run, y))


def forward(sums, params, keep, pre, count, blocks, pieces, step=512):
    parts = params.shape[1]
    rows = pre.shape[0] // parts
    each = rows // pieces // step
    width = parts * 128 // blocks

    def piece(n):
        return pl.BlockSpec((blocks, step, width), lambda i: (0, jnp.clip(i - n * each, 0, each - 1), 0))

    return pl.pallas_call(
        functools.partial(forward_kernel, count),
        grid=(rows // step,),
        in_specs=[
            pl.BlockSpec(sums.shape, lambda i: (0, 0, 0)),
            pl.BlockSpec(params.shape, lambda i: (0, 0, 0)),
            whole(pltpu.SMEM),
            pl.BlockSpec((step * parts, 128), lambda i: (i, 0)),
        ],
        out_specs=[pl.BlockSpec((step * parts, 128), lambda i: (i, 0))] + [piece(n) for n in range(pieces)],
        out_shape=[jax.ShapeDtypeStruct(pre.shape, f32)]
        + [jax.ShapeDtypeStruct((blocks, rows // pieces, width), bf16)] * pieces,
        scratch_shapes=[pltpu.VMEM((parts, 128), f32)],
        compiler_params=pltpu.CompilerParams(vmem_limit_bytes=BIG),
        cost_estimate=pl.CostEstimate(flops=12 * pre.size, bytes_accessed=10 * pre.size, transcendentals=pre.size),
    )(sums, params, keep, pre)


def backward_kernel(count, terms, sums, params, keep, pre, states, before, *rest):
    dys, (carried, totals, slots, held) = rest[:-4], rest[-4:]
    mean, _, rstd = stats_of(sums, count)
    shift = -mean * rstd
    decay = params[2]
    parts = decay.shape[0]
    rows, width = dys[0].shape[1:]
    groups = rows // 16
    per = width // 128
    pieces = [dys[n : n + terms] for n in range(0, len(dys), terms)]
    blocks = pl.num_programs(0)
    block = blocks - 1 - pl.program_id(0)
    first = block * rows

    @pl.when(pl.program_id(0) == 0)
    def _():
        held[...] = jnp.zeros_like(held)

    def turn(g, slot):
        at = pl.ds(pl.multiple_of(g * 16, 16), 16)
        for k in range(parts):
            lane = k % per * 128
            value = None
            for n, piece in enumerate(pieces):
                v = piece[0][k // per, at, lane : lane + 128].astype(f32)
                for d in piece[1:]:
                    v = v + d[k // per, at, lane : lane + 128].astype(f32)
                value = v if value is None else jnp.where(block >= n * (blocks // len(pieces)), v, value)
            for u in range(2):
                slots[slot, pl.ds(u * 8 * parts + k, 8, stride=parts), :] = value[u * 8 : u * 8 + 8]

    def scan(g, slot, carry, begin=None):
        for u in range(15, -1, -1):
            back, sg, sx, sd = carry
            t = g * 16 + u
            at = pl.ds(pl.multiple_of(t * parts, parts), parts)
            h = states[at, :]
            s = 1.0 / (1.0 + jnp.exp(-h))
            dy = slots[slot, u * parts : u * parts + parts, :]
            value = dy * (s + h * s * (1.0 - s)) + back
            carried[at, :] = value
            k = keep[first + t]
            if begin is not None and u == 0:
                prior = begin
            else:
                prior = states[pl.ds(pl.multiple_of((t - 1) * parts, parts), parts), :]
            carry = (
                (decay * k) * value,
                sg + value,
                sx + value * (pre[at, :] * rstd + shift),
                sd + (value * k) * prior,
            )
        return carry

    def two(i, carry):
        g = groups - 1 - 2 * i
        turn(g - 1, 1)
        carry = scan(g, 0, carry)
        turn(g - 2, 0)
        return scan(g - 1, 1, carry)

    turn(groups - 1, 0)
    carry = lax.fori_loop(0, groups // 2 - 1, two, (held[0], held[1], held[2], held[3]))
    turn(0, 1)
    carry = scan(1, 0, carry)
    begin = jnp.where(block == 0, jnp.zeros_like(decay), before[...])
    carry = scan(0, 1, carry, begin)
    for n in range(4):
        held[n] = carry[n]
    totals[0], totals[1], totals[2] = carry[1], carry[2], carry[3]


def backward(sums, params, keep, pre, states, dys, terms, count, step=256):
    parts = params.shape[1]
    rows = pre.shape[0] // parts
    last = rows // step - 1
    blocks, _, width = dys[0].shape
    pieces = len(dys) // terms
    each = rows // pieces // step

    def piece(n):
        return pl.BlockSpec((blocks, step, width), lambda i: (0, jnp.clip(last - i - n * each, 0, each - 1), 0))

    long = pl.BlockSpec((step * parts, 128), lambda i: (last - i, 0))
    return pl.pallas_call(
        functools.partial(backward_kernel, count, terms),
        grid=(rows // step,),
        in_specs=[
            pl.BlockSpec(sums.shape, lambda i: (0, 0, 0)),
            pl.BlockSpec(params.shape, lambda i: (0, 0, 0)),
            whole(pltpu.SMEM),
            long,
            long,
            pl.BlockSpec((parts, 128), lambda i: (jnp.maximum((last - i) * step - 1, 0), 0)),
        ]
        + [piece(n // terms) for n in range(len(dys))],
        out_specs=[long, pl.BlockSpec((3, parts, 128), lambda i: (0, 0, 0))],
        out_shape=[
            jax.ShapeDtypeStruct(pre.shape, f32),
            jax.ShapeDtypeStruct((3, parts, 128), f32),
        ],
        scratch_shapes=[pltpu.VMEM((2, 16 * parts, 128), f32), pltpu.VMEM((4, parts, 128), f32)],
        compiler_params=pltpu.CompilerParams(vmem_limit_bytes=BIG),
        cost_estimate=pl.CostEstimate(flops=24 * pre.size, bytes_accessed=16 * pre.size, transcendentals=pre.size),
    )(sums, params, keep, pre, states, states, *dys)


def times_side(d, w, out, by_row, side=0):
    dims = (((1,), (1,)), ((), ()))
    blocks, _, width = out.shape
    for r in range(blocks):
        acc = None
        for z in range(blocks):
            piece = d[:, z * width : z * width + width]
            term = lax.dot_general(piece, tile_of(w, r, z, side, by_row), dims, preferred_element_type=f32)
            acc = term if acc is None else acc + term
        out[r] = acc.astype(out.dtype)


def side_of(w, side):
    return pl.BlockSpec(w.shape[:2] + (1,) + w.shape[3:], lambda i: (0, 0, side, 0, 0))


def spread_kernel(count, by_row, sums, params, totals, carried, pre, w, dpre, *outs):
    mean, _, rstd = stats_of(sums, count)
    sc = params[0] * rstd
    slope = sc * rstd * (totals[1] / count)
    c3 = mean * slope - sc * (totals[0] / count)
    parts = sc.shape[0]
    for g in range(dpre.shape[0] // 16):
        for k in range(parts):
            both = []
            for u in range(2):
                at = pl.ds((g * 16 + u * 8) * parts + k, 8, stride=parts)
                both.append(sc[k : k + 1] * carried[at, :] - slope[k : k + 1] * pre[at, :] + c3[k : k + 1])
            dpre[g * 16 : g * 16 + 16, k * 128 : k * 128 + 128] = jnp.concatenate(both, 0).astype(bf16)
    for side, out in enumerate(outs):
        times_side(dpre, w, out, by_row, side)


def spread(sums, params, totals, carried, pre, w, by_row, count, sides, step=512):
    parts = params.shape[1]
    rows, cols = pre.shape[0] // parts, parts * 128
    blocks, width = w.shape[0], w.shape[4]
    return pl.pallas_call(
        functools.partial(spread_kernel, count, by_row),
        grid=(rows // step,),
        in_specs=[
            pl.BlockSpec(sums.shape, lambda i: (0, 0, 0)),
            pl.BlockSpec(params.shape, lambda i: (0, 0, 0)),
            pl.BlockSpec(totals.shape, lambda i: (0, 0, 0)),
            pl.BlockSpec((step * parts, 128), lambda i: (i, 0)),
            pl.BlockSpec((step * parts, 128), lambda i: (i, 0)),
            side_of(w, 1) if sides == 1 else pl.BlockSpec(w.shape, lambda i: (0, 0, 0, 0, 0)),
        ],
        out_specs=[pl.BlockSpec((step, cols), lambda i: (i, 0))]
        + [pl.BlockSpec((blocks, step, width), lambda i: (0, i, 0))] * sides,
        out_shape=[jax.ShapeDtypeStruct((rows, cols), bf16)]
        + [jax.ShapeDtypeStruct((blocks, rows, width), bf16)] * sides,
        compiler_params=pltpu.CompilerParams(vmem_limit_bytes=BIG),
        cost_estimate=pl.CostEstimate(flops=2 * sides * rows * cols * cols, bytes_accessed=16 << 20, transcendentals=0),
    )(sums, params, totals, carried, pre, w)


def spread_own_kernel(by_row, dpre, w, same):
    times_side(dpre, w, same, by_row)


def spread_own(dpre, w, by_row, step=512):
    rows, cols = dpre.shape
    blocks, width = w.shape[0], w.shape[4]
    return pl.pallas_call(
        functools.partial(spread_own_kernel, by_row),
        grid=(rows // step,),
        in_specs=[pl.BlockSpec((step, cols), lambda i: (i, 0)), side_of(w, 0)],
        out_specs=pl.BlockSpec((blocks, step, width), lambda i: (0, i, 0)),
        out_shape=jax.ShapeDtypeStruct((blocks, rows, width), bf16),
        compiler_params=pltpu.CompilerParams(vmem_limit_bytes=BIG),
        cost_estimate=pl.CostEstimate(flops=2 * rows * cols * cols, bytes_accessed=6 << 20, transcendentals=0),
    )(dpre, w)


def load_kernel(same, other, late, out):
    rows = same.shape[1]
    out[0, :rows, :] = (same[0].astype(f32) + other[0].astype(f32)).astype(out.dtype)
    out[0, rows:, :] = late[0]


def load(same, other, late):
    blocks, rows, width = same.shape
    more = late.shape[1]
    return pl.pallas_call(
        load_kernel,
        grid=(blocks,),
        in_specs=[
            pl.BlockSpec((1, rows, width), lambda i: (i, 0, 0)),
            pl.BlockSpec((1, rows, width), lambda i: (i, 0, 0)),
            pl.BlockSpec((1, more, width), lambda i: (i, 0, 0)),
        ],
        out_specs=pl.BlockSpec((1, rows + more, width), lambda i: (i, 0, 0)),
        out_shape=jax.ShapeDtypeStruct((blocks, rows + more, width), bf16),
        compiler_params=pltpu.CompilerParams(vmem_limit_bytes=BIG),
        cost_estimate=pl.CostEstimate(flops=0, bytes_accessed=8 << 20, transcendentals=0),
    )(same, other, late)


def outer_kernel(by_row, xs, xo, dpre, out):
    width = xs.shape[2]
    dims = (((0,), (0,)), ((), ()))
    for side, x in enumerate((xs, xo)):
        term = lax.dot_general(x[0], dpre[...], dims, preferred_element_type=f32).astype(bf16)
        for z in range(dpre.shape[1] // width):
            piece = term[:, z * width : z * width + width]
            if by_row:
                out[0, z, side] = piece
            else:
                out[z, 0, side] = piece


def outer(xs, xo, dpre, by_row):
    blocks, rows, width = xs.shape
    tile = (1, blocks, 2, width, width) if by_row else (blocks, 1, 2, width, width)
    return pl.pallas_call(
        functools.partial(outer_kernel, by_row),
        grid=(blocks,),
        in_specs=[
            pl.BlockSpec((1, rows, width), lambda i: (i, 0, 0)),
            pl.BlockSpec((1, rows, width), lambda i: (i, 0, 0)),
            pl.BlockSpec(dpre.shape, lambda i: (0, 0)),
        ],
        out_specs=pl.BlockSpec(tile, (lambda i: (i, 0, 0, 0, 0)) if by_row else (lambda i: (0, i, 0, 0, 0))),
        out_shape=jax.ShapeDtypeStruct((blocks, blocks, 2, width, width), bf16),
        compiler_params=pltpu.CompilerParams(vmem_limit_bytes=BIG),
        cost_estimate=pl.CostEstimate(flops=4 * rows * dpre.shape[1] ** 2, bytes_accessed=10 << 20, transcendentals=0),
    )(xs, xo, dpre)


def place_kernel(core, mine, theirs, *rest):
    out = rest[-1]
    half = out.shape[1] // 2
    c = core[0]
    out[:, pl.ds(pl.multiple_of(c * half, half), half)] = mine[0].astype(out.dtype)
    out[:, pl.ds(pl.multiple_of((1 - c) * half, half), half)] = theirs[0].astype(out.dtype)


def place(core, mine, theirs, kind, piece, pieces, before):
    count, length, half = theirs.shape
    spec = pl.BlockSpec((length, 2 * half), lambda i, core: (i * pieces + piece, 0))
    prior = [] if before is None else [before]
    return pl.pallas_call(
        place_kernel,
        grid_spec=pltpu.PrefetchScalarGridSpec(
            num_scalar_prefetch=1,
            grid=(count,),
            in_specs=[
                pl.BlockSpec((1, length, half), lambda i, core: (core[0] * count + i, 0, 0)),
                pl.BlockSpec((1, length, half), lambda i, core: (i, 0, 0)),
            ]
            + [pl.BlockSpec(memory_space=pl.ANY)] * len(prior),
            out_specs=spec,
        ),
        out_shape=jax.ShapeDtypeStruct((count * length * pieces, 2 * half), kind),
        input_output_aliases={3: 0} if prior else {},
        compiler_params=pltpu.CompilerParams(vmem_limit_bytes=BIG),
        cost_estimate=pl.CostEstimate(flops=0, bytes_accessed=6 << 20, transcendentals=0),
    )(core, mine, theirs, *prior)


def paired(frames, weights, gains, shifts, decays, resets, running, grad_out):
    wide, narrow = lax.axis_size("wide"), lax.axis_size(NARROW)
    rows, lanes = frames.shape
    half = lanes // 2
    depth = weights.shape[1]
    count = rows * narrow * 1.0
    z = lax.axis_index("wide")
    r, c = lax.axis_index("ring"), lax.axis_index("core")

    def send(x, to):
        pairs = []
        for a in range(wide):
            for b in range(narrow):
                tz, tr, tc = to(a, b // 2, b % 2)
                pairs.append((a * narrow + b, tz * narrow + tr * 2 + tc))
        return lax.ppermute(x, AXES, pairs)

    def swap(x):
        return send(x, lambda a, b, d: (a, b, 1 - d))

    def over_ring(x, m):
        return send(x, lambda a, b, d: (a, b ^ m, d))

    def over_wide(x, m):
        return send(x, lambda a, b, d: (a ^ m, b, d))

    def everywhere(x, extra=None):
        a1, a2, a3 = over_ring(x, 1), over_ring(x, 2), over_ring(x, 3)
        x = (x + a1) + (a2 + a3)
        if extra is None:
            a1, a2, a3 = over_wide(x, 1), over_wide(x, 2), over_wide(x, 3)
            return (x + a1) + (a2 + a3)
        load = jnp.concatenate([x.reshape(-1, 128), extra])
        got = [over_wide(load, m) for m in range(1, wide)]
        a1, a2, a3 = (g[: x.size // 128].reshape(x.shape) for g in got)
        return (x + a1) + (a2 + a3), [extra] + [g[x.size // 128 :] for g in got]

    def placed(pieces, shape, spots):
        buf = jnp.zeros(shape, pieces[0].dtype)
        for piece, spot in zip(pieces, spots, strict=True):
            buf = lax.dynamic_update_slice(buf, piece, spot)
        return buf

    def by_half(x, first, length):
        x = x.reshape(wide // 2, LENGTH, lanes)[:, first : first + length]
        mine = lax.dynamic_slice(x, (0, 0, c * half), (wide // 2, length, half))
        theirs = swap(lax.dynamic_slice(x, (0, 0, (1 - c) * half), (wide // 2, length, half)))
        return jnp.concatenate([jnp.where(c == 0, mine, theirs), jnp.where(c == 0, theirs, mine)])

    def exchange(x):
        return lax.all_to_all(x, "wide", 0, 0, tiled=True)

    def others(mine):
        return swap(lax.dynamic_slice_in_dim(mine, (1 - c) * (wide // 2), wide // 2, 0))

    def halves(w):
        axis = w.ndim - 1
        own = lax.dynamic_slice_in_dim(w, c * half, half, axis)
        return own, swap(lax.dynamic_slice_in_dim(w, (1 - c) * half, half, axis))

    def along_ring(line):
        pieces = [line] + [over_ring(line, m) for m in range(1, 4)]
        return placed([p[None] for p in pieces], (4,) + line.shape, [(r ^ m,) + (0,) * line.ndim for m in range(4)])

    def gathered_late(both):
        return lax.all_gather(lax.all_gather(both, "wide"), "ring")

    def ring_pieces(tiles):
        pieces = [lax.dynamic_index_in_dim(tiles, r ^ m, 0, keepdims=False) for m in range(4)]
        return pieces[:1] + [over_ring(pieces[m], m) for m in range(1, 4)]

    def rows_late(tiles):
        return lax.psum_scatter(tiles.reshape(4 * wide * 2, depth, half), "ring", scatter_dimension=0, tiled=True)

    theirs = swap(resets)
    row = jnp.where(c == z // 2, resets, theirs)
    keep = 1.0 - lax.dynamic_slice(row, ((z % 2) * LENGTH,), (LENGTH,)).astype(f32)
    vectors = jnp.concatenate([gains, shifts, decays])
    vectors = lax.dynamic_slice(vectors, (0, c * half), (6, half)).reshape(-1, 128)

    second = jnp.stack(halves(weights[1]))
    shards = [weights[0]] + [over_wide(weights[0], m) for m in range(1, wide)]
    x = by_half(frames, 0, LENGTH)
    cut = LENGTH // 2
    x, shards, keep, grad_out, second = lax.optimization_barrier((x, shards, keep, grad_out, second))
    mats = [None, gathered_late(second)]
    xs = exchange(x)
    line = jnp.stack(halves(jnp.stack(shards)), 1)
    line = placed([line[m][None] for m in range(wide)], line.shape, [(z ^ m, 0, 0, 0) for m in range(wide)])
    mats[0] = along_ring(line)
    g_early, g_late = by_half(grad_out, 0, cut), by_half(grad_out, cut, cut)
    xs, mats[0], g_late = lax.optimization_barrier((xs, mats[0], g_late))
    xo = swap(xs)
    g_late = exchange(g_late)

    saved = []
    ins = (xs, xo)
    for level in range(2):
        pre, sums = product(*ins, mats[level], True)
        if level == 0:
            sums, pieces = everywhere(sums, vectors)
            spots = [(0, (z ^ m) * half) for m in range(wide)]
            vectors = placed([p.reshape(6, half) for p in pieces], (6, wide * half), spots)
            vectors = vectors.reshape(3, 2, -1, 128)
            params = [vectors[:, i] for i in range(2)]
            sums, g_late, g_early = lax.optimization_barrier((sums, g_late, g_early))
            g_early = exchange(g_early)
        else:
            sums = everywhere(sums)
        states, *y = forward(sums, params[level], keep, pre, count, wide, 1 + level)
        saved.append((ins, pre, sums, states))
        if level == 0:
            ins = (y[0], swap(y[0]))
    out_early = exchange(y[0])

    core = c.reshape(1)
    dys, terms = (g_early, g_late), 1
    totals_list = [None, None]
    for level in (1, 0):
        ins, pre, sums, states = saved[level]
        carried, totals = backward(sums, params[level], keep, pre, states, dys, terms, count)
        totals = everywhere(totals)
        totals_list[level] = totals
        if level:
            out_early, out_late, totals = lax.optimization_barrier((out_early, y[1], totals))
            out_late = exchange(out_late)
        else:
            out_early, out_late, totals = lax.optimization_barrier((out_early, out_late, totals))
        back_of = functools.partial(spread, sums, params[level], totals, carried, pre, mats[level], True, count)
        if level:
            dpre, other = back_of(1)
            other = swap(other)
            tiles = outer(*ins, dpre, True)
            tiles, dpre = lax.optimization_barrier((tiles, dpre))
            late = rows_late(tiles)
            dys, terms = (spread_own(dpre, mats[level], True), other), 2
        else:
            dpre, other = back_of(1)
            other = swap(other)
            same = spread_own(dpre, mats[level], True)
            both = exchange(load(same, other, late.reshape(wide, 2 * depth, half)))
            tiles = outer(*ins, dpre, True)
            sent = place(core, out_early, others(out_early), bf16, 0, 2, None)
            sent = place(core, out_late, others(out_late), bf16, 1, 2, sent)
            pieces, sent = lax.optimization_barrier((ring_pieces(tiles), sent))
            pieces = [p.astype(f32) for p in pieces]
            line = ((pieces[0] + pieces[1]) + (pieces[2] + pieces[3])).astype(bf16)
            own, away = line[:, 0], swap(line[:, 1])
            line = jnp.concatenate([jnp.where(c == 0, own, away), jnp.where(c == 0, away, own)], axis=2)
            line, both = lax.optimization_barrier((line, both))
            line = exchange(line)
            back = place(core, both, others(both[:, :LENGTH]), f32, 0, 1, None)
            late = jnp.sum(both[:, LENGTH:].astype(f32), 0).reshape(2, depth, half)
            own, away = late[0], swap(late[1])
            late = jnp.concatenate([jnp.where(c == 0, own, away), jnp.where(c == 0, away, own)], axis=1)
            line, back, late = lax.optimization_barrier((line, back, late))
            weight_grad = jnp.stack([jnp.sum(line.astype(f32), 0), late])

    small = []
    for level in range(2):
        mean, var, _ = stats_of(saved[level][2], count)
        small.append(jnp.concatenate([mean[None], var[None], totals_list[level]]))
    small = jnp.stack(small).reshape(2, 5, wide, half)
    small = lax.dynamic_index_in_dim(small, z, 2, keepdims=False)
    away = swap(small)
    small = jnp.concatenate([jnp.where(c == 0, small, away), jnp.where(c == 0, away, small)], axis=2)
    new_mean = (1.0 - momentum) * running[:, 0] + momentum * small[:, 0]
    new_var = (1.0 - momentum) * running[:, 1] + momentum * small[:, 1] * count / (count - 1.0)
    return (
        sent,
        back,
        weight_grad,
        small[:, 3],
        small[:, 2],
        small[:, 4],
        jnp.stack([new_mean, new_var], axis=1),
    )


def link(earlier, later):
    return (earlier[0] * later[0], later[0] * earlier[1] + later[1])


def general(frames, weights, gains, shifts, decays, resets, running, grad_out):
    frame_rows, lanes = frames.shape
    count = frame_rows * lax.axis_size(NARROW) * 1.0
    keep = (1 - resets).astype(jnp.float32).reshape(-1, LENGTH, 1)
    layer_in = frames
    saved = []
    updated = []
    for level in range(2):
        full_in = lax.all_gather(layer_in, "wide", axis=1, tiled=True)
        full_weight = lax.all_gather(weights[level], NARROW, axis=0, tiled=True)
        pre = jnp.dot(full_in, full_weight, preferred_element_type=jnp.float32)
        total, squares = lax.psum((jnp.sum(pre, 0), jnp.sum(pre * pre, 0)), NARROW)
        mean = total / count
        var = squares / count - mean * mean
        scale = lax.rsqrt(var + eps_norm)
        normed_hat = (pre - mean) * scale
        drive = (normed_hat * gains[level] + shifts[level]).reshape(-1, LENGTH, lanes)
        rate = keep * decays[level]
        _, states = lax.associative_scan(link, (rate, drive), axis=1)
        saved.append((full_in, full_weight, normed_hat, scale, states, rate))
        states = states.reshape(frame_rows, lanes)
        layer_in = jax.nn.silu(states).astype(jnp.bfloat16)
        new_mean = (1.0 - momentum) * running[level, 0] + momentum * mean
        new_var = (1.0 - momentum) * running[level, 1] + momentum * var * count / (count - 1.0)
        updated.append(jnp.stack([new_mean, new_var]))
    grad = grad_out.astype(jnp.float32)
    weight_list = [None, None]
    gain_list = [None, None]
    shift_list = [None, None]
    decay_list = [None, None]
    for level in (1, 0):
        full_in, full_weight, normed_hat, scale, states, rate = saved[level]
        sigma = jax.nn.sigmoid(states)
        grad_state = grad.reshape(-1, LENGTH, lanes) * (sigma + states * sigma * (1.0 - sigma))
        rate_next = jnp.concatenate([rate[:, 1:], jnp.zeros_like(rate[:, :1])], axis=1)
        _, carried = lax.associative_scan(link, (rate_next, grad_state), reverse=True, axis=1)
        prior = jnp.concatenate([jnp.zeros_like(states[:, :1]), states[:, :-1]], axis=1)
        decay_term = jnp.sum(carried * keep * prior, axis=(0, 1))
        carried = carried.reshape(frame_rows, lanes)
        shift_sum, gain_sum, decay_sum = lax.psum(
            (jnp.sum(carried, 0), jnp.sum(carried * normed_hat, 0), decay_term), NARROW
        )
        grad_pre = (
            gains[level] * scale * (carried - shift_sum / count - normed_hat * gain_sum / count)
        ).astype(jnp.bfloat16)
        weight_list[level] = lax.psum_scatter(
            lax.dot_general(
                full_in, grad_pre, (((0,), (0,)), ((), ())), preferred_element_type=jnp.float32
            ),
            NARROW,
            scatter_dimension=0,
            tiled=True,
        )
        gain_list[level] = gain_sum
        shift_list[level] = shift_sum
        decay_list[level] = decay_sum
        partial_term = lax.dot_general(
            grad_pre, full_weight, (((1,), (1,)), ((), ())), preferred_element_type=jnp.float32
        )
        grad = lax.psum_scatter(partial_term, "wide", scatter_dimension=1, tiled=True)
    return (
        layer_in,
        grad,
        jnp.stack(weight_list),
        jnp.stack(gain_list),
        jnp.stack(shift_list),
        jnp.stack(decay_list),
        jnp.stack(updated),
    )


def per_device(frames, weights, *rest):
    wide, narrow = lax.axis_size("wide"), lax.axis_size(NARROW)
    rows, lanes = frames.shape
    one_row_a_chip = 2 * rows == wide * LENGTH and wide == 4 and narrow == 2 * wide
    if one_row_a_chip and lanes == 2 * weights.shape[1] and wide * lanes == 2048:
        return paired(frames, weights, *rest)
    return general(frames, weights, *rest)


def solution(mesh):
    wide, narrow = mesh.shape["wide"], mesh.shape["narrow"]
    devices = mesh.devices if mesh.axis_names == ("wide", "narrow") else mesh.devices.T
    cut = Mesh(devices.reshape(wide, narrow // 2, 2), AXES)
    placed = (
        P(NARROW, "wide"),
        P(None, NARROW, "wide"),
        P(None, "wide"),
        P(None, "wide"),
        P(None, "wide"),
        P(NARROW),
        P(None, None, "wide"),
        P(NARROW, "wide"),
    )
    return jax.shard_map(
        per_device,
        mesh=cut,
        in_specs=placed,
        out_specs=(
            P(NARROW, "wide"),
            P(NARROW, "wide"),
            P(None, NARROW, "wide"),
            P(None, "wide"),
            P(None, "wide"),
            P(None, "wide"),
            P(None, None, "wide"),
        ),
        check_vma=False,
    )
```

```python
import functools

import jax
import jax.numpy as jnp
from jax import lax
from jax.experimental import pallas as pl
from jax.experimental.pallas import tpu as pltpu
from jax.sharding import Mesh
from jax.sharding import PartitionSpec as P

LENGTH = 1024


eps_norm = 1e-05
momentum = 0.1

f32 = jnp.float32
bf16 = jnp.bfloat16
BIG = 56 * 2**20
AXES = ("wide", "ring", "core")
NARROW = ("ring", "core")


def whole(space=pltpu.VMEM):
    return pl.BlockSpec(memory_space=space)


def stats_of(sums, count):
    mean = sums[0] / count
    var = sums[1] / count - mean * mean
    return mean, var, lax.rsqrt(var + eps_norm)


def tile_of(w, r, z, side, by_row):
    return w[r, z, side] if by_row else w[z, r, side]


def product_kernel(by_row, xs, xo, w, pre, sums):
    blocks, rows, width = xs.shape
    per = width // 128
    parts = blocks * per

    @pl.when(pl.program_id(0) == 0)
    def _():
        sums[...] = jnp.zeros_like(sums)

    for z in range(blocks):
        acc = None
        for side, x in enumerate((xs, xo)):
            for r in range(blocks):
                term = jnp.dot(x[r], tile_of(w, r, z, side, by_row), preferred_element_type=f32)
                acc = term if acc is None else acc + term
        for k in range(per):
            piece = acc[:, k * 128 : k * 128 + 128]
            at = z * per + k
            for g in range(rows // 8):
                pre[pl.ds(g * 8 * parts + at, 8, stride=parts), :] = piece[g * 8 : g * 8 + 8]
            sums[0, at : at + 1, :] += jnp.sum(piece, 0, keepdims=True)
            sums[1, at : at + 1, :] += jnp.sum(piece * piece, 0, keepdims=True)


def product(xs, xo, w, by_row, step=256):
    blocks, rows, width = xs.shape
    cols = blocks * width
    parts = cols // 128
    return pl.pallas_call(
        functools.partial(product_kernel, by_row),
        grid=(rows // step,),
        in_specs=[
            pl.BlockSpec((blocks, step, width), lambda i: (0, i, 0)),
            pl.BlockSpec((blocks, step, width), lambda i: (0, i, 0)),
            pl.BlockSpec(w.shape, lambda i: (0, 0, 0, 0, 0)),
        ],
        out_specs=[
            pl.BlockSpec((step * parts, 128), lambda i: (i, 0)),
            pl.BlockSpec((2, parts, 128), lambda i: (0, 0, 0)),
        ],
        out_shape=[
            jax.ShapeDtypeStruct((rows * parts, 128), f32),
            jax.ShapeDtypeStruct((2, parts, 128), f32),
        ],
        compiler_params=pltpu.CompilerParams(vmem_limit_bytes=BIG),
        cost_estimate=pl.CostEstimate(flops=4 * rows * cols * cols, bytes_accessed=12 << 20, transcendentals=0),
    )(xs, xo, w)


def forward_kernel(count, sums, params, keep, pre, states, *rest):
    ys, held = rest[:-1], rest[-1]
    mean, _, rstd = stats_of(sums, count)
    sc = params[0] * rstd
    sh = params[1] - mean * sc
    decay = params[2]
    parts = sc.shape[0]
    rows, width = ys[0].shape[1:]
    per = width // 128
    groups = rows // 16
    block, blocks = pl.program_id(0), pl.num_programs(0)
    first = block * rows

    @pl.when(block == 0)
    def _():
        held[...] = jnp.zeros_like(held)

    def scan(g, h):
        for u in range(16):
            t = g * 16 + u
            at = pl.ds(pl.multiple_of(t * parts, parts), parts)
            h = (decay * keep[first + t]) * h + (pre[at, :] * sc + sh)
            states[at, :] = h
        return h

    def turn(y, g):
        for k in range(parts):
            two = []
            for u in range(2):
                h = states[pl.ds((g * 16 + u * 8) * parts + k, 8, stride=parts), :]
                two.append(h / (1.0 + jnp.exp(-h)))
            lane = k % per * 128
            at = pl.ds(pl.multiple_of(g * 16, 16), 16)
            y[k // per, at, lane : lane + 128] = jnp.concatenate(two, 0).astype(bf16)

    def run(y):
        def both(g, h):
            turn(y, g - 1)
            return scan(g, h)

        held[...] = lax.fori_loop(1, groups, both, scan(0, held[...]))
        turn(y, groups - 1)

    for n, y in enumerate(ys):
        pl.when(block // (blocks // len(ys)) == n)(functools.partial(run, y))


def forward(sums, params, keep, pre, count, blocks, pieces, step=512):
    parts = params.shape[1]
    rows = pre.shape[0] // parts
    each = rows // pieces // step
    width = parts * 128 // blocks

    def piece(n):
        return pl.BlockSpec((blocks, step, width), lambda i: (0, jnp.clip(i - n * each, 0, each - 1), 0))

    return pl.pallas_call(
        functools.partial(forward_kernel, count),
        grid=(rows // step,),
        in_specs=[
            pl.BlockSpec(sums.shape, lambda i: (0, 0, 0)),
            pl.BlockSpec(params.shape, lambda i: (0, 0, 0)),
            whole(pltpu.SMEM),
            pl.BlockSpec((step * parts, 128), lambda i: (i, 0)),
        ],
        out_specs=[pl.BlockSpec((step * parts, 128), lambda i: (i, 0))] + [piece(n) for n in range(pieces)],
        out_shape=[jax.ShapeDtypeStruct(pre.shape, f32)]
        + [jax.ShapeDtypeStruct((blocks, rows // pieces, width), bf16)] * pieces,
        scratch_shapes=[pltpu.VMEM((parts, 128), f32)],
        compiler_params=pltpu.CompilerParams(vmem_limit_bytes=BIG),
        cost_estimate=pl.CostEstimate(flops=12 * pre.size, bytes_accessed=10 * pre.size, transcendentals=pre.size),
    )(sums, params, keep, pre)


def backward_kernel(count, terms, sums, params, keep, pre, states, before, *rest):
    dys, (carried, totals, slots, held) = rest[:-4], rest[-4:]
    mean, _, rstd = stats_of(sums, count)
    shift = -mean * rstd
    decay = params[2]
    parts = decay.shape[0]
    rows, width = dys[0].shape[1:]
    groups = rows // 16
    per = width // 128
    pieces = [dys[n : n + terms] for n in range(0, len(dys), terms)]
    blocks = pl.num_programs(0)
    block = blocks - 1 - pl.program_id(0)
    first = block * rows

    @pl.when(pl.program_id(0) == 0)
    def _():
        held[...] = jnp.zeros_like(held)

    def turn(g, slot):
        at = pl.ds(pl.multiple_of(g * 16, 16), 16)
        for k in range(parts):
            lane = k % per * 128
            value = None
            for n, piece in enumerate(pieces):
                v = piece[0][k // per, at, lane : lane + 128].astype(f32)
                for d in piece[1:]:
                    v = v + d[k // per, at, lane : lane + 128].astype(f32)
                value = v if value is None else jnp.where(block >= n * (blocks // len(pieces)), v, value)
            for u in range(2):
                slots[slot, pl.ds(u * 8 * parts + k, 8, stride=parts), :] = value[u * 8 : u * 8 + 8]

    def scan(g, slot, carry, begin=None):
        for u in range(15, -1, -1):
            back, sg, sx, sd = carry
            t = g * 16 + u
            at = pl.ds(pl.multiple_of(t * parts, parts), parts)
            h = states[at, :]
            s = 1.0 / (1.0 + jnp.exp(-h))
            dy = slots[slot, u * parts : u * parts + parts, :]
            value = dy * (s + h * s * (1.0 - s)) + back
            carried[at, :] = value
            k = keep[first + t]
            if begin is not None and u == 0:
                prior = begin
            else:
                prior = states[pl.ds(pl.multiple_of((t - 1) * parts, parts), parts), :]
            carry = (
                (decay * k) * value,
                sg + value,
                sx + value * (pre[at, :] * rstd + shift),
                sd + (value * k) * prior,
            )
        return carry

    def two(i, carry):
        g = groups - 1 - 2 * i
        turn(g - 1, 1)
        carry = scan(g, 0, carry)
        turn(g - 2, 0)
        return scan(g - 1, 1, carry)

    turn(groups - 1, 0)
    carry = lax.fori_loop(0, groups // 2 - 1, two, (held[0], held[1], held[2], held[3]))
    turn(0, 1)
    carry = scan(1, 0, carry)
    begin = jnp.where(block == 0, jnp.zeros_like(decay), before[...])
    carry = scan(0, 1, carry, begin)
    for n in range(4):
        held[n] = carry[n]
    totals[0], totals[1], totals[2] = carry[1], carry[2], carry[3]


def backward(sums, params, keep, pre, states, dys, terms, count, step=256):
    parts = params.shape[1]
    rows = pre.shape[0] // parts
    last = rows // step - 1
    blocks, _, width = dys[0].shape
    pieces = len(dys) // terms
    each = rows // pieces // step

    def piece(n):
        return pl.BlockSpec((blocks, step, width), lambda i: (0, jnp.clip(last - i - n * each, 0, each - 1), 0))

    long = pl.BlockSpec((step * parts, 128), lambda i: (last - i, 0))
    return pl.pallas_call(
        functools.partial(backward_kernel, count, terms),
        grid=(rows // step,),
        in_specs=[
            pl.BlockSpec(sums.shape, lambda i: (0, 0, 0)),
            pl.BlockSpec(params.shape, lambda i: (0, 0, 0)),
            whole(pltpu.SMEM),
            long,
            long,
            pl.BlockSpec((parts, 128), lambda i: (jnp.maximum((last - i) * step - 1, 0), 0)),
        ]
        + [piece(n // terms) for n in range(len(dys))],
        out_specs=[long, pl.BlockSpec((3, parts, 128), lambda i: (0, 0, 0))],
        out_shape=[
            jax.ShapeDtypeStruct(pre.shape, f32),
            jax.ShapeDtypeStruct((3, parts, 128), f32),
        ],
        scratch_shapes=[pltpu.VMEM((2, 16 * parts, 128), f32), pltpu.VMEM((4, parts, 128), f32)],
        compiler_params=pltpu.CompilerParams(vmem_limit_bytes=BIG),
        cost_estimate=pl.CostEstimate(flops=24 * pre.size, bytes_accessed=16 * pre.size, transcendentals=pre.size),
    )(sums, params, keep, pre, states, states, *dys)


def times_side(d, w, out, by_row, side=0):
    dims = (((1,), (1,)), ((), ()))
    blocks, _, width = out.shape
    for r in range(blocks):
        acc = None
        for z in range(blocks):
            piece = d[:, z * width : z * width + width]
            term = lax.dot_general(piece, tile_of(w, r, z, side, by_row), dims, preferred_element_type=f32)
            acc = term if acc is None else acc + term
        out[r] = acc.astype(out.dtype)


def side_of(w, side):
    return pl.BlockSpec(w.shape[:2] + (1,) + w.shape[3:], lambda i: (0, 0, side, 0, 0))


def spread_kernel(count, by_row, sums, params, totals, carried, pre, w, dpre, *outs):
    mean, _, rstd = stats_of(sums, count)
    sc = params[0] * rstd
    slope = sc * rstd * (totals[1] / count)
    c3 = mean * slope - sc * (totals[0] / count)
    parts = sc.shape[0]
    for g in range(dpre.shape[0] // 16):
        for k in range(parts):
            both = []
            for u in range(2):
                at = pl.ds((g * 16 + u * 8) * parts + k, 8, stride=parts)
                both.append(sc[k : k + 1] * carried[at, :] - slope[k : k + 1] * pre[at, :] + c3[k : k + 1])
            dpre[g * 16 : g * 16 + 16, k * 128 : k * 128 + 128] = jnp.concatenate(both, 0).astype(bf16)
    for side, out in enumerate(outs):
        times_side(dpre, w, out, by_row, side)


def spread(sums, params, totals, carried, pre, w, by_row, count, sides, step=512):
    parts = params.shape[1]
    rows, cols = pre.shape[0] // parts, parts * 128
    blocks, width = w.shape[0], w.shape[4]
    return pl.pallas_call(
        functools.partial(spread_kernel, count, by_row),
        grid=(rows // step,),
        in_specs=[
            pl.BlockSpec(sums.shape, lambda i: (0, 0, 0)),
            pl.BlockSpec(params.shape, lambda i: (0, 0, 0)),
            pl.BlockSpec(totals.shape, lambda i: (0, 0, 0)),
            pl.BlockSpec((step * parts, 128), lambda i: (i, 0)),
            pl.BlockSpec((step * parts, 128), lambda i: (i, 0)),
            side_of(w, 1) if sides == 1 else pl.BlockSpec(w.shape, lambda i: (0, 0, 0, 0, 0)),
        ],
        out_specs=[pl.BlockSpec((step, cols), lambda i: (i, 0))]
        + [pl.BlockSpec((blocks, step, width), lambda i: (0, i, 0))] * sides,
        out_shape=[jax.ShapeDtypeStruct((rows, cols), bf16)]
        + [jax.ShapeDtypeStruct((blocks, rows, width), bf16)] * sides,
        compiler_params=pltpu.CompilerParams(vmem_limit_bytes=BIG),
        cost_estimate=pl.CostEstimate(flops=2 * sides * rows * cols * cols, bytes_accessed=16 << 20, transcendentals=0),
    )(sums, params, totals, carried, pre, w)


def spread_own_kernel(by_row, dpre, w, same):
    times_side(dpre, w, same, by_row)


def spread_own(dpre, w, by_row, step=512):
    rows, cols = dpre.shape
    blocks, width = w.shape[0], w.shape[4]
    return pl.pallas_call(
        functools.partial(spread_own_kernel, by_row),
        grid=(rows // step,),
        in_specs=[pl.BlockSpec((step, cols), lambda i: (i, 0)), side_of(w, 0)],
        out_specs=pl.BlockSpec((blocks, step, width), lambda i: (0, i, 0)),
        out_shape=jax.ShapeDtypeStruct((blocks, rows, width), bf16),
        compiler_params=pltpu.CompilerParams(vmem_limit_bytes=BIG),
        cost_estimate=pl.CostEstimate(flops=2 * rows * cols * cols, bytes_accessed=6 << 20, transcendentals=0),
    )(dpre, w)


def load_kernel(same, other, late, out):
    rows = same.shape[1]
    out[0, :rows, :] = (same[0].astype(f32) + other[0].astype(f32)).astype(out.dtype)
    out[0, rows:, :] = late[0]


def load(same, other, late):
    blocks, rows, width = same.shape
    more = late.shape[1]
    return pl.pallas_call(
        load_kernel,
        grid=(blocks,),
        in_specs=[
            pl.BlockSpec((1, rows, width), lambda i: (i, 0, 0)),
            pl.BlockSpec((1, rows, width), lambda i: (i, 0, 0)),
            pl.BlockSpec((1, more, width), lambda i: (i, 0, 0)),
        ],
        out_specs=pl.BlockSpec((1, rows + more, width), lambda i: (i, 0, 0)),
        out_shape=jax.ShapeDtypeStruct((blocks, rows + more, width), bf16),
        compiler_params=pltpu.CompilerParams(vmem_limit_bytes=BIG),
        cost_estimate=pl.CostEstimate(flops=0, bytes_accessed=8 << 20, transcendentals=0),
    )(same, other, late)


def outer_kernel(by_row, xs, xo, dpre, out):
    width = xs.shape[2]
    dims = (((0,), (0,)), ((), ()))
    for side, x in enumerate((xs, xo)):
        term = lax.dot_general(x[0], dpre[...], dims, preferred_element_type=f32).astype(bf16)
        for z in range(dpre.shape[1] // width):
            piece = term[:, z * width : z * width + width]
            if by_row:
                out[0, z, side] = piece
            else:
                out[z, 0, side] = piece


def outer(xs, xo, dpre, by_row):
    blocks, rows, width = xs.shape
    tile = (1, blocks, 2, width, width) if by_row else (blocks, 1, 2, width, width)
    return pl.pallas_call(
        functools.partial(outer_kernel, by_row),
        grid=(blocks,),
        in_specs=[
            pl.BlockSpec((1, rows, width), lambda i: (i, 0, 0)),
            pl.BlockSpec((1, rows, width), lambda i: (i, 0, 0)),
            pl.BlockSpec(dpre.shape, lambda i: (0, 0)),
        ],
        out_specs=pl.BlockSpec(tile, (lambda i: (i, 0, 0, 0, 0)) if by_row else (lambda i: (0, i, 0, 0, 0))),
        out_shape=jax.ShapeDtypeStruct((blocks, blocks, 2, width, width), bf16),
        compiler_params=pltpu.CompilerParams(vmem_limit_bytes=BIG),
        cost_estimate=pl.CostEstimate(flops=4 * rows * dpre.shape[1] ** 2, bytes_accessed=10 << 20, transcendentals=0),
    )(xs, xo, dpre)


def place_kernel(core, mine, theirs, *rest):
    out = rest[-1]
    half = out.shape[1] // 2
    c = core[0]
    out[:, pl.ds(pl.multiple_of(c * half, half), half)] = mine[0].astype(out.dtype)
    out[:, pl.ds(pl.multiple_of((1 - c) * half, half), half)] = theirs[0].astype(out.dtype)


def place(core, mine, theirs, kind, piece, pieces, before):
    count, length, half = theirs.shape
    spec = pl.BlockSpec((length, 2 * half), lambda i, core: (i * pieces + piece, 0))
    prior = [] if before is None else [before]
    return pl.pallas_call(
        place_kernel,
        grid_spec=pltpu.PrefetchScalarGridSpec(
            num_scalar_prefetch=1,
            grid=(count,),
            in_specs=[
                pl.BlockSpec((1, length, half), lambda i, core: (core[0] * count + i, 0, 0)),
                pl.BlockSpec((1, length, half), lambda i, core: (i, 0, 0)),
            ]
            + [pl.BlockSpec(memory_space=pl.ANY)] * len(prior),
            out_specs=spec,
        ),
        out_shape=jax.ShapeDtypeStruct((count * length * pieces, 2 * half), kind),
        input_output_aliases={3: 0} if prior else {},
        compiler_params=pltpu.CompilerParams(vmem_limit_bytes=BIG),
        cost_estimate=pl.CostEstimate(flops=0, bytes_accessed=6 << 20, transcendentals=0),
    )(core, mine, theirs, *prior)


def paired(frames, weights, gains, shifts, decays, resets, running, grad_out):
    wide, narrow = lax.axis_size("wide"), lax.axis_size(NARROW)
    rows, lanes = frames.shape
    half = lanes // 2
    depth = weights.shape[1]
    count = rows * narrow * 1.0
    z = lax.axis_index("wide")
    r, c = lax.axis_index("ring"), lax.axis_index("core")

    def send(x, to):
        pairs = []
        for a in range(wide):
            for b in range(narrow):
                tz, tr, tc = to(a, b // 2, b % 2)
                pairs.append((a * narrow + b, tz * narrow + tr * 2 + tc))
        return lax.ppermute(x, AXES, pairs)

    def swap(x):
        return send(x, lambda a, b, d: (a, b, 1 - d))

    def over_ring(x, m):
        return send(x, lambda a, b, d: (a, b ^ m, d))

    def over_wide(x, m):
        return send(x, lambda a, b, d: (a ^ m, b, d))

    def everywhere(x, extra=None):
        a1, a2, a3 = over_ring(x, 1), over_ring(x, 2), over_ring(x, 3)
        x = (x + a1) + (a2 + a3)
        if extra is None:
            a1, a2, a3 = over_wide(x, 1), over_wide(x, 2), over_wide(x, 3)
            return (x + a1) + (a2 + a3)
        load = jnp.concatenate([x.reshape(-1, 128), extra])
        got = [over_wide(load, m) for m in range(1, wide)]
        a1, a2, a3 = (g[: x.size // 128].reshape(x.shape) for g in got)
        return (x + a1) + (a2 + a3), [extra] + [g[x.size // 128 :] for g in got]

    def placed(pieces, shape, spots):
        buf = jnp.zeros(shape, pieces[0].dtype)
        for piece, spot in zip(pieces, spots, strict=True):
            buf = lax.dynamic_update_slice(buf, piece, spot)
        return buf

    def by_half(x, first, length):
        x = x.reshape(wide // 2, LENGTH, lanes)[:, first : first + length]
        mine = lax.dynamic_slice(x, (0, 0, c * half), (wide // 2, length, half))
        theirs = swap(lax.dynamic_slice(x, (0, 0, (1 - c) * half), (wide // 2, length, half)))
        return jnp.concatenate([jnp.where(c == 0, mine, theirs), jnp.where(c == 0, theirs, mine)])

    def exchange(x):
        return lax.all_to_all(x, "wide", 0, 0, tiled=True)

    def others(mine):
        return swap(lax.dynamic_slice_in_dim(mine, (1 - c) * (wide // 2), wide // 2, 0))

    def halves(w):
        axis = w.ndim - 1
        own = lax.dynamic_slice_in_dim(w, c * half, half, axis)
        return own, swap(lax.dynamic_slice_in_dim(w, (1 - c) * half, half, axis))

    def along_ring(line):
        pieces = [line] + [over_ring(line, m) for m in range(1, 4)]
        return placed([p[None] for p in pieces], (4,) + line.shape, [(r ^ m,) + (0,) * line.ndim for m in range(4)])

    def gathered_late(both):
        return lax.all_gather(lax.all_gather(both, "wide"), "ring")

    def ring_pieces(tiles):
        pieces = [lax.dynamic_index_in_dim(tiles, r ^ m, 0, keepdims=False) for m in range(4)]
        return pieces[:1] + [over_ring(pieces[m], m) for m in range(1, 4)]

    def rows_late(tiles):
        return lax.psum_scatter(tiles.reshape(4 * wide * 2, depth, half), "ring", scatter_dimension=0, tiled=True)

    theirs = swap(resets)
    row = jnp.where(c == z // 2, resets, theirs)
    keep = 1.0 - lax.dynamic_slice(row, ((z % 2) * LENGTH,), (LENGTH,)).astype(f32)
    vectors = jnp.concatenate([gains, shifts, decays])
    vectors = lax.dynamic_slice(vectors, (0, c * half), (6, half)).reshape(-1, 128)

    second = jnp.stack(halves(weights[1]))
    shards = [weights[0]] + [over_wide(weights[0], m) for m in range(1, wide)]
    x = by_half(frames, 0, LENGTH)
    cut = LENGTH // 2
    x, shards[2], keep = lax.optimization_barrier((x, shards[2], keep))
    shards[3], second = lax.optimization_barrier((shards[3], second))
    shards, grad_out = lax.optimization_barrier((shards, grad_out))
    mats = [None, gathered_late(second)]
    xs = exchange(x)
    line = jnp.stack(halves(jnp.stack(shards)), 1)
    line = placed([line[m][None] for m in range(wide)], line.shape, [(z ^ m, 0, 0, 0) for m in range(wide)])
    mats[0] = along_ring(line)
    g_early, g_late = by_half(grad_out, 0, cut), by_half(grad_out, cut, cut)
    xs, mats[0], g_late = lax.optimization_barrier((xs, mats[0], g_late))
    xo = swap(xs)
    g_late = exchange(g_late)

    saved = []
    ins = (xs, xo)
    for level in range(2):
        pre, sums = product(*ins, mats[level], True)
        if level == 0:
            sums, pieces = everywhere(sums, vectors)
            spots = [(0, (z ^ m) * half) for m in range(wide)]
            vectors = placed([p.reshape(6, half) for p in pieces], (6, wide * half), spots)
            vectors = vectors.reshape(3, 2, -1, 128)
            params = [vectors[:, i] for i in range(2)]
            sums, g_late, g_early = lax.optimization_barrier((sums, g_late, g_early))
            g_early = exchange(g_early)
        else:
            sums = everywhere(sums)
        states, *y = forward(sums, params[level], keep, pre, count, wide, 1 + level)
        saved.append((ins, pre, sums, states))
        if level == 0:
            ins = (y[0], swap(y[0]))
    out_early = exchange(y[0])

    core = c.reshape(1)
    dys, terms = (g_early, g_late), 1
    totals_list = [None, None]
    for level in (1, 0):
        ins, pre, sums, states = saved[level]
        carried, totals = backward(sums, params[level], keep, pre, states, dys, terms, count)
        totals = everywhere(totals)
        totals_list[level] = totals
        if level:
            out_early, out_late, totals = lax.optimization_barrier((out_early, y[1], totals))
            out_late = exchange(out_late)
        else:
            out_early, out_late, totals = lax.optimization_barrier((out_early, out_late, totals))
        back_of = functools.partial(spread, sums, params[level], totals, carried, pre, mats[level], True, count)
        if level:
            dpre, other = back_of(1)
            other = swap(other)
            tiles = outer(*ins, dpre, True)
            tiles, dpre = lax.optimization_barrier((tiles, dpre))
            late = rows_late(tiles)
            dys, terms = (spread_own(dpre, mats[level], True), other), 2
        else:
            dpre, other = back_of(1)
            other = swap(other)
            same = spread_own(dpre, mats[level], True)
            both = exchange(load(same, other, late.reshape(wide, 2 * depth, half)))
            tiles = outer(*ins, dpre, True)
            sent = place(core, out_early, others(out_early), bf16, 0, 2, None)
            sent = place(core, out_late, others(out_late), bf16, 1, 2, sent)
            pieces, sent = lax.optimization_barrier((ring_pieces(tiles), sent))
            pieces = [p.astype(f32) for p in pieces]
            line = ((pieces[0] + pieces[1]) + (pieces[2] + pieces[3])).astype(bf16)
            own, away = line[:, 0], swap(line[:, 1])
            line = jnp.concatenate([jnp.where(c == 0, own, away), jnp.where(c == 0, away, own)], axis=2)
            line, both = lax.optimization_barrier((line, both))
            line = exchange(line)
            back = place(core, both, others(both[:, :LENGTH]), f32, 0, 1, None)
            late = jnp.sum(both[:, LENGTH:].astype(f32), 0).reshape(2, depth, half)
            own, away = late[0], swap(late[1])
            late = jnp.concatenate([jnp.where(c == 0, own, away), jnp.where(c == 0, away, own)], axis=1)
            line, back, late = lax.optimization_barrier((line, back, late))
            weight_grad = jnp.stack([jnp.sum(line.astype(f32), 0), late])

    small = []
    for level in range(2):
        mean, var, _ = stats_of(saved[level][2], count)
        small.append(jnp.concatenate([mean[None], var[None], totals_list[level]]))
    small = jnp.stack(small).reshape(2, 5, wide, half)
    small = lax.dynamic_index_in_dim(small, z, 2, keepdims=False)
    away = swap(small)
    small = jnp.concatenate([jnp.where(c == 0, small, away), jnp.where(c == 0, away, small)], axis=2)
    new_mean = (1.0 - momentum) * running[:, 0] + momentum * small[:, 0]
    new_var = (1.0 - momentum) * running[:, 1] + momentum * small[:, 1] * count / (count - 1.0)
    return (
        sent,
        back,
        weight_grad,
        small[:, 3],
        small[:, 2],
        small[:, 4],
        jnp.stack([new_mean, new_var], axis=1),
    )


def link(earlier, later):
    return (earlier[0] * later[0], later[0] * earlier[1] + later[1])


def general(frames, weights, gains, shifts, decays, resets, running, grad_out):
    frame_rows, lanes = frames.shape
    count = frame_rows * lax.axis_size(NARROW) * 1.0
    keep = (1 - resets).astype(jnp.float32).reshape(-1, LENGTH, 1)
    layer_in = frames
    saved = []
    updated = []
    for level in range(2):
        full_in = lax.all_gather(layer_in, "wide", axis=1, tiled=True)
        full_weight = lax.all_gather(weights[level], NARROW, axis=0, tiled=True)
        pre = jnp.dot(full_in, full_weight, preferred_element_type=jnp.float32)
        total, squares = lax.psum((jnp.sum(pre, 0), jnp.sum(pre * pre, 0)), NARROW)
        mean = total / count
        var = squares / count - mean * mean
        scale = lax.rsqrt(var + eps_norm)
        normed_hat = (pre - mean) * scale
        drive = (normed_hat * gains[level] + shifts[level]).reshape(-1, LENGTH, lanes)
        rate = keep * decays[level]
        _, states = lax.associative_scan(link, (rate, drive), axis=1)
        saved.append((full_in, full_weight, normed_hat, scale, states, rate))
        states = states.reshape(frame_rows, lanes)
        layer_in = jax.nn.silu(states).astype(jnp.bfloat16)
        new_mean = (1.0 - momentum) * running[level, 0] + momentum * mean
        new_var = (1.0 - momentum) * running[level, 1] + momentum * var * count / (count - 1.0)
        updated.append(jnp.stack([new_mean, new_var]))
    grad = grad_out.astype(jnp.float32)
    weight_list = [None, None]
    gain_list = [None, None]
    shift_list = [None, None]
    decay_list = [None, None]
    for level in (1, 0):
        full_in, full_weight, normed_hat, scale, states, rate = saved[level]
        sigma = jax.nn.sigmoid(states)
        grad_state = grad.reshape(-1, LENGTH, lanes) * (sigma + states * sigma * (1.0 - sigma))
        rate_next = jnp.concatenate([rate[:, 1:], jnp.zeros_like(rate[:, :1])], axis=1)
        _, carried = lax.associative_scan(link, (rate_next, grad_state), reverse=True, axis=1)
        prior = jnp.concatenate([jnp.zeros_like(states[:, :1]), states[:, :-1]], axis=1)
        decay_term = jnp.sum(carried * keep * prior, axis=(0, 1))
        carried = carried.reshape(frame_rows, lanes)
        shift_sum, gain_sum, decay_sum = lax.psum(
            (jnp.sum(carried, 0), jnp.sum(carried * normed_hat, 0), decay_term), NARROW
        )
        grad_pre = (
            gains[level] * scale * (carried - shift_sum / count - normed_hat * gain_sum / count)
        ).astype(jnp.bfloat16)
        weight_list[level] = lax.psum_scatter(
            lax.dot_general(
                full_in, grad_pre, (((0,), (0,)), ((), ())), preferred_element_type=jnp.float32
            ),
            NARROW,
            scatter_dimension=0,
            tiled=True,
        )
        gain_list[level] = gain_sum
        shift_list[level] = shift_sum
        decay_list[level] = decay_sum
        partial_term = lax.dot_general(
            grad_pre, full_weight, (((1,), (1,)), ((), ())), preferred_element_type=jnp.float32
        )
        grad = lax.psum_scatter(partial_term, "wide", scatter_dimension=1, tiled=True)
    return (
        layer_in,
        grad,
        jnp.stack(weight_list),
        jnp.stack(gain_list),
        jnp.stack(shift_list),
        jnp.stack(decay_list),
        jnp.stack(updated),
    )


def per_device(frames, weights, *rest):
    wide, narrow = lax.axis_size("wide"), lax.axis_size(NARROW)
    rows, lanes = frames.shape
    one_row_a_chip = 2 * rows == wide * LENGTH and wide == 4 and narrow == 2 * wide
    if one_row_a_chip and lanes == 2 * weights.shape[1] and wide * lanes == 2048:
        return paired(frames, weights, *rest)
    return general(frames, weights, *rest)


def solution(mesh):
    wide, narrow = mesh.shape["wide"], mesh.shape["narrow"]
    devices = mesh.devices if mesh.axis_names == ("wide", "narrow") else mesh.devices.T
    cut = Mesh(devices.reshape(wide, narrow // 2, 2), AXES)
    placed = (
        P(NARROW, "wide"),
        P(None, NARROW, "wide"),
        P(None, "wide"),
        P(None, "wide"),
        P(None, "wide"),
        P(NARROW),
        P(None, None, "wide"),
        P(NARROW, "wide"),
    )
    return jax.shard_map(
        per_device,
        mesh=cut,
        in_specs=placed,
        out_specs=(
            P(NARROW, "wide"),
            P(NARROW, "wide"),
            P(None, NARROW, "wide"),
            P(None, "wide"),
            P(None, "wide"),
            P(None, "wide"),
            P(None, None, "wide"),
        ),
        check_vma=False,
    )
```

```python
import functools

import jax
import jax.numpy as jnp
from jax import lax
from jax.experimental import pallas as pl
from jax.experimental.pallas import tpu as pltpu
from jax.sharding import Mesh
from jax.sharding import PartitionSpec as P

LENGTH = 1024


eps_norm = 1e-05
momentum = 0.1

f32 = jnp.float32
bf16 = jnp.bfloat16
BIG = 56 * 2**20
AXES = ("wide", "ring", "core")
NARROW = ("ring", "core")


def whole(space=pltpu.VMEM):
    return pl.BlockSpec(memory_space=space)


def stats_of(sums, count):
    mean = sums[0] / count
    var = sums[1] / count - mean * mean
    return mean, var, lax.rsqrt(var + eps_norm)


def tile_of(w, r, z, side, by_row):
    return w[r, z, side] if by_row else w[z, r, side]


def product_kernel(by_row, xs, xo, w, pre, sums):
    blocks, rows, width = xs.shape
    per = width // 128
    parts = blocks * per

    @pl.when(pl.program_id(0) == 0)
    def _():
        sums[...] = jnp.zeros_like(sums)

    for z in range(blocks):
        acc = None
        for side, x in enumerate((xs, xo)):
            for r in range(blocks):
                term = jnp.dot(x[r], tile_of(w, r, z, side, by_row), preferred_element_type=f32)
                acc = term if acc is None else acc + term
        for k in range(per):
            piece = acc[:, k * 128 : k * 128 + 128]
            at = z * per + k
            for g in range(rows // 8):
                pre[pl.ds(g * 8 * parts + at, 8, stride=parts), :] = piece[g * 8 : g * 8 + 8]
            sums[0, at : at + 1, :] += jnp.sum(piece, 0, keepdims=True)
            sums[1, at : at + 1, :] += jnp.sum(piece * piece, 0, keepdims=True)


def product(xs, xo, w, by_row, step=256):
    blocks, rows, width = xs.shape
    cols = blocks * width
    parts = cols // 128
    return pl.pallas_call(
        functools.partial(product_kernel, by_row),
        grid=(rows // step,),
        in_specs=[
            pl.BlockSpec((blocks, step, width), lambda i: (0, i, 0)),
            pl.BlockSpec((blocks, step, width), lambda i: (0, i, 0)),
            pl.BlockSpec(w.shape, lambda i: (0, 0, 0, 0, 0)),
        ],
        out_specs=[
            pl.BlockSpec((step * parts, 128), lambda i: (i, 0)),
            pl.BlockSpec((2, parts, 128), lambda i: (0, 0, 0)),
        ],
        out_shape=[
            jax.ShapeDtypeStruct((rows * parts, 128), f32),
            jax.ShapeDtypeStruct((2, parts, 128), f32),
        ],
        compiler_params=pltpu.CompilerParams(vmem_limit_bytes=BIG),
        cost_estimate=pl.CostEstimate(flops=4 * rows * cols * cols, bytes_accessed=12 << 20, transcendentals=0),
    )(xs, xo, w)


def forward_kernel(count, sums, params, keep, pre, states, *rest):
    ys, held = rest[:-1], rest[-1]
    mean, _, rstd = stats_of(sums, count)
    sc = params[0] * rstd
    sh = params[1] - mean * sc
    decay = params[2]
    parts = sc.shape[0]
    rows, width = ys[0].shape[1:]
    per = width // 128
    groups = rows // 16
    block, blocks = pl.program_id(0), pl.num_programs(0)
    first = block * rows

    @pl.when(block == 0)
    def _():
        held[...] = jnp.zeros_like(held)

    def scan(g, h):
        for u in range(16):
            t = g * 16 + u
            at = pl.ds(pl.multiple_of(t * parts, parts), parts)
            h = (decay * keep[first + t]) * h + (pre[at, :] * sc + sh)
            states[at, :] = h
        return h

    def turn(y, g):
        for k in range(parts):
            two = []
            for u in range(2):
                h = states[pl.ds((g * 16 + u * 8) * parts + k, 8, stride=parts), :]
                two.append(h / (1.0 + jnp.exp(-h)))
            lane = k % per * 128
            at = pl.ds(pl.multiple_of(g * 16, 16), 16)
            y[k // per, at, lane : lane + 128] = jnp.concatenate(two, 0).astype(bf16)

    def run(y):
        def both(g, h):
            turn(y, g - 1)
            return scan(g, h)

        held[...] = lax.fori_loop(1, groups, both, scan(0, held[...]))
        turn(y, groups - 1)

    for n, y in enumerate(ys):
        pl.when(block // (blocks // len(ys)) == n)(functools.partial(run, y))


def forward(sums, params, keep, pre, count, blocks, pieces, step=512):
    parts = params.shape[1]
    rows = pre.shape[0] // parts
    each = rows // pieces // step
    width = parts * 128 // blocks

    def piece(n):
        return pl.BlockSpec((blocks, step, width), lambda i: (0, jnp.clip(i - n * each, 0, each - 1), 0))

    return pl.pallas_call(
        functools.partial(forward_kernel, count),
        grid=(rows // step,),
        in_specs=[
            pl.BlockSpec(sums.shape, lambda i: (0, 0, 0)),
            pl.BlockSpec(params.shape, lambda i: (0, 0, 0)),
            whole(pltpu.SMEM),
            pl.BlockSpec((step * parts, 128), lambda i: (i, 0)),
        ],
        out_specs=[pl.BlockSpec((step * parts, 128), lambda i: (i, 0))] + [piece(n) for n in range(pieces)],
        out_shape=[jax.ShapeDtypeStruct(pre.shape, f32)]
        + [jax.ShapeDtypeStruct((blocks, rows // pieces, width), bf16)] * pieces,
        scratch_shapes=[pltpu.VMEM((parts, 128), f32)],
        compiler_params=pltpu.CompilerParams(vmem_limit_bytes=BIG),
        cost_estimate=pl.CostEstimate(flops=12 * pre.size, bytes_accessed=10 * pre.size, transcendentals=pre.size),
    )(sums, params, keep, pre)


def backward_kernel(count, terms, sums, params, keep, pre, states, before, *rest):
    dys, (carried, totals, slots, held) = rest[:-4], rest[-4:]
    mean, _, rstd = stats_of(sums, count)
    shift = -mean * rstd
    decay = params[2]
    parts = decay.shape[0]
    rows, width = dys[0].shape[1:]
    groups = rows // 16
    per = width // 128
    pieces = [dys[n : n + terms] for n in range(0, len(dys), terms)]
    blocks = pl.num_programs(0)
    block = blocks - 1 - pl.program_id(0)
    first = block * rows

    @pl.when(pl.program_id(0) == 0)
    def _():
        held[...] = jnp.zeros_like(held)

    def turn(g, slot):
        at = pl.ds(pl.multiple_of(g * 16, 16), 16)
        for k in range(parts):
            lane = k % per * 128
            value = None
            for n, piece in enumerate(pieces):
                v = piece[0][k // per, at, lane : lane + 128].astype(f32)
                for d in piece[1:]:
                    v = v + d[k // per, at, lane : lane + 128].astype(f32)
                value = v if value is None else jnp.where(block >= n * (blocks // len(pieces)), v, value)
            for u in range(2):
                slots[slot, pl.ds(u * 8 * parts + k, 8, stride=parts), :] = value[u * 8 : u * 8 + 8]

    def scan(g, slot, carry, begin=None):
        for u in range(15, -1, -1):
            back, sg, sx, sd = carry
            t = g * 16 + u
            at = pl.ds(pl.multiple_of(t * parts, parts), parts)
            h = states[at, :]
            s = 1.0 / (1.0 + jnp.exp(-h))
            dy = slots[slot, u * parts : u * parts + parts, :]
            value = dy * (s + h * s * (1.0 - s)) + back
            carried[at, :] = value
            k = keep[first + t]
            if begin is not None and u == 0:
                prior = begin
            else:
                prior = states[pl.ds(pl.multiple_of((t - 1) * parts, parts), parts), :]
            carry = (
                (decay * k) * value,
                sg + value,
                sx + value * (pre[at, :] * rstd + shift),
                sd + (value * k) * prior,
            )
        return carry

    def two(i, carry):
        g = groups - 1 - 2 * i
        turn(g - 1, 1)
        carry = scan(g, 0, carry)
        turn(g - 2, 0)
        return scan(g - 1, 1, carry)

    turn(groups - 1, 0)
    carry = lax.fori_loop(0, groups // 2 - 1, two, (held[0], held[1], held[2], held[3]))
    turn(0, 1)
    carry = scan(1, 0, carry)
    begin = jnp.where(block == 0, jnp.zeros_like(decay), before[...])
    carry = scan(0, 1, carry, begin)
    for n in range(4):
        held[n] = carry[n]
    totals[0], totals[1], totals[2] = carry[1], carry[2], carry[3]


def backward(sums, params, keep, pre, states, dys, terms, count, step=256):
    parts = params.shape[1]
    rows = pre.shape[0] // parts
    last = rows // step - 1
    blocks, _, width = dys[0].shape
    pieces = len(dys) // terms
    each = rows // pieces // step

    def piece(n):
        return pl.BlockSpec((blocks, step, width), lambda i: (0, jnp.clip(last - i - n * each, 0, each - 1), 0))

    long = pl.BlockSpec((step * parts, 128), lambda i: (last - i, 0))
    return pl.pallas_call(
        functools.partial(backward_kernel, count, terms),
        grid=(rows // step,),
        in_specs=[
            pl.BlockSpec(sums.shape, lambda i: (0, 0, 0)),
            pl.BlockSpec(params.shape, lambda i: (0, 0, 0)),
            whole(pltpu.SMEM),
            long,
            long,
            pl.BlockSpec((parts, 128), lambda i: (jnp.maximum((last - i) * step - 1, 0), 0)),
        ]
        + [piece(n // terms) for n in range(len(dys))],
        out_specs=[long, pl.BlockSpec((3, parts, 128), lambda i: (0, 0, 0))],
        out_shape=[
            jax.ShapeDtypeStruct(pre.shape, f32),
            jax.ShapeDtypeStruct((3, parts, 128), f32),
        ],
        scratch_shapes=[pltpu.VMEM((2, 16 * parts, 128), f32), pltpu.VMEM((4, parts, 128), f32)],
        compiler_params=pltpu.CompilerParams(vmem_limit_bytes=BIG),
        cost_estimate=pl.CostEstimate(flops=24 * pre.size, bytes_accessed=16 * pre.size, transcendentals=pre.size),
    )(sums, params, keep, pre, states, states, *dys)


def times_side(d, w, out, by_row, side=0):
    dims = (((1,), (1,)), ((), ()))
    blocks, _, width = out.shape
    for r in range(blocks):
        acc = None
        for z in range(blocks):
            piece = d[:, z * width : z * width + width]
            term = lax.dot_general(piece, tile_of(w, r, z, side, by_row), dims, preferred_element_type=f32)
            acc = term if acc is None else acc + term
        out[r] = acc.astype(out.dtype)


def side_of(w, side):
    return pl.BlockSpec(w.shape[:2] + (1,) + w.shape[3:], lambda i: (0, 0, side, 0, 0))


def spread_kernel(count, by_row, sums, params, totals, carried, pre, w, dpre, *outs):
    mean, _, rstd = stats_of(sums, count)
    sc = params[0] * rstd
    slope = sc * rstd * (totals[1] / count)
    c3 = mean * slope - sc * (totals[0] / count)
    parts = sc.shape[0]
    for g in range(dpre.shape[0] // 16):
        for k in range(parts):
            both = []
            for u in range(2):
                at = pl.ds((g * 16 + u * 8) * parts + k, 8, stride=parts)
                both.append(sc[k : k + 1] * carried[at, :] - slope[k : k + 1] * pre[at, :] + c3[k : k + 1])
            dpre[g * 16 : g * 16 + 16, k * 128 : k * 128 + 128] = jnp.concatenate(both, 0).astype(bf16)
    for side, out in enumerate(outs):
        times_side(dpre, w, out, by_row, side)


def spread(sums, params, totals, carried, pre, w, by_row, count, sides, step=512):
    parts = params.shape[1]
    rows, cols = pre.shape[0] // parts, parts * 128
    blocks, width = w.shape[0], w.shape[4]
    return pl.pallas_call(
        functools.partial(spread_kernel, count, by_row),
        grid=(rows // step,),
        in_specs=[
            pl.BlockSpec(sums.shape, lambda i: (0, 0, 0)),
            pl.BlockSpec(params.shape, lambda i: (0, 0, 0)),
            pl.BlockSpec(totals.shape, lambda i: (0, 0, 0)),
            pl.BlockSpec((step * parts, 128), lambda i: (i, 0)),
            pl.BlockSpec((step * parts, 128), lambda i: (i, 0)),
            side_of(w, 1) if sides == 1 else pl.BlockSpec(w.shape, lambda i: (0, 0, 0, 0, 0)),
        ],
        out_specs=[pl.BlockSpec((step, cols), lambda i: (i, 0))]
        + [pl.BlockSpec((blocks, step, width), lambda i: (0, i, 0))] * sides,
        out_shape=[jax.ShapeDtypeStruct((rows, cols), bf16)]
        + [jax.ShapeDtypeStruct((blocks, rows, width), bf16)] * sides,
        compiler_params=pltpu.CompilerParams(vmem_limit_bytes=BIG),
        cost_estimate=pl.CostEstimate(flops=2 * sides * rows * cols * cols, bytes_accessed=16 << 20, transcendentals=0),
    )(sums, params, totals, carried, pre, w)


def spread_own_kernel(by_row, dpre, w, same):
    times_side(dpre, w, same, by_row)


def spread_own(dpre, w, by_row, step=512):
    rows, cols = dpre.shape
    blocks, width = w.shape[0], w.shape[4]
    return pl.pallas_call(
        functools.partial(spread_own_kernel, by_row),
        grid=(rows // step,),
        in_specs=[pl.BlockSpec((step, cols), lambda i: (i, 0)), side_of(w, 0)],
        out_specs=pl.BlockSpec((blocks, step, width), lambda i: (0, i, 0)),
        out_shape=jax.ShapeDtypeStruct((blocks, rows, width), bf16),
        compiler_params=pltpu.CompilerParams(vmem_limit_bytes=BIG),
        cost_estimate=pl.CostEstimate(flops=2 * rows * cols * cols, bytes_accessed=6 << 20, transcendentals=0),
    )(dpre, w)


def load_kernel(same, other, late, out):
    rows = same.shape[1]
    out[0, :rows, :] = (same[0].astype(f32) + other[0].astype(f32)).astype(out.dtype)
    out[0, rows:, :] = late[0]


def load(same, other, late):
    blocks, rows, width = same.shape
    more = late.shape[1]
    return pl.pallas_call(
        load_kernel,
        grid=(blocks,),
        in_specs=[
            pl.BlockSpec((1, rows, width), lambda i: (i, 0, 0)),
            pl.BlockSpec((1, rows, width), lambda i: (i, 0, 0)),
            pl.BlockSpec((1, more, width), lambda i: (i, 0, 0)),
        ],
        out_specs=pl.BlockSpec((1, rows + more, width), lambda i: (i, 0, 0)),
        out_shape=jax.ShapeDtypeStruct((blocks, rows + more, width), bf16),
        compiler_params=pltpu.CompilerParams(vmem_limit_bytes=BIG),
        cost_estimate=pl.CostEstimate(flops=0, bytes_accessed=8 << 20, transcendentals=0),
    )(same, other, late)


def outer_kernel(by_row, xs, xo, dpre, out):
    width = xs.shape[2]
    dims = (((0,), (0,)), ((), ()))
    for side, x in enumerate((xs, xo)):
        term = lax.dot_general(x[0], dpre[...], dims, preferred_element_type=f32).astype(bf16)
        for z in range(dpre.shape[1] // width):
            piece = term[:, z * width : z * width + width]
            if by_row:
                out[0, z, side] = piece
            else:
                out[z, 0, side] = piece


def outer(xs, xo, dpre, by_row):
    blocks, rows, width = xs.shape
    tile = (1, blocks, 2, width, width) if by_row else (blocks, 1, 2, width, width)
    return pl.pallas_call(
        functools.partial(outer_kernel, by_row),
        grid=(blocks,),
        in_specs=[
            pl.BlockSpec((1, rows, width), lambda i: (i, 0, 0)),
            pl.BlockSpec((1, rows, width), lambda i: (i, 0, 0)),
            pl.BlockSpec(dpre.shape, lambda i: (0, 0)),
        ],
        out_specs=pl.BlockSpec(tile, (lambda i: (i, 0, 0, 0, 0)) if by_row else (lambda i: (0, i, 0, 0, 0))),
        out_shape=jax.ShapeDtypeStruct((blocks, blocks, 2, width, width), bf16),
        compiler_params=pltpu.CompilerParams(vmem_limit_bytes=BIG),
        cost_estimate=pl.CostEstimate(flops=4 * rows * dpre.shape[1] ** 2, bytes_accessed=10 << 20, transcendentals=0),
    )(xs, xo, dpre)


def place_kernel(core, mine, theirs, *rest):
    out = rest[-1]
    half = out.shape[1] // 2
    c = core[0]
    out[:, pl.ds(pl.multiple_of(c * half, half), half)] = mine[0].astype(out.dtype)
    out[:, pl.ds(pl.multiple_of((1 - c) * half, half), half)] = theirs[0].astype(out.dtype)


def place(core, mine, theirs, kind, piece, pieces, before):
    count, length, half = theirs.shape
    spec = pl.BlockSpec((length, 2 * half), lambda i, core: (i * pieces + piece, 0))
    prior = [] if before is None else [before]
    return pl.pallas_call(
        place_kernel,
        grid_spec=pltpu.PrefetchScalarGridSpec(
            num_scalar_prefetch=1,
            grid=(count,),
            in_specs=[
                pl.BlockSpec((1, length, half), lambda i, core: (core[0] * count + i, 0, 0)),
                pl.BlockSpec((1, length, half), lambda i, core: (i, 0, 0)),
            ]
            + [pl.BlockSpec(memory_space=pl.ANY)] * len(prior),
            out_specs=spec,
        ),
        out_shape=jax.ShapeDtypeStruct((count * length * pieces, 2 * half), kind),
        input_output_aliases={3: 0} if prior else {},
        compiler_params=pltpu.CompilerParams(vmem_limit_bytes=BIG),
        cost_estimate=pl.CostEstimate(flops=0, bytes_accessed=6 << 20, transcendentals=0),
    )(core, mine, theirs, *prior)


def paired(frames, weights, gains, shifts, decays, resets, running, grad_out):
    wide, narrow = lax.axis_size("wide"), lax.axis_size(NARROW)
    rows, lanes = frames.shape
    half = lanes // 2
    depth = weights.shape[1]
    count = rows * narrow * 1.0
    z = lax.axis_index("wide")
    r, c = lax.axis_index("ring"), lax.axis_index("core")

    def send(x, to):
        pairs = []
        for a in range(wide):
            for b in range(narrow):
                tz, tr, tc = to(a, b // 2, b % 2)
                pairs.append((a * narrow + b, tz * narrow + tr * 2 + tc))
        return lax.ppermute(x, AXES, pairs)

    def swap(x):
        return send(x, lambda a, b, d: (a, b, 1 - d))

    def over_ring(x, m):
        return send(x, lambda a, b, d: (a, b ^ m, d))

    def over_wide(x, m):
        return send(x, lambda a, b, d: (a ^ m, b, d))

    def everywhere(x, extra=None):
        a1, a2, a3 = over_ring(x, 1), over_ring(x, 2), over_ring(x, 3)
        x = (x + a1) + (a2 + a3)
        if extra is None:
            a1, a2, a3 = over_wide(x, 1), over_wide(x, 2), over_wide(x, 3)
            return (x + a1) + (a2 + a3)
        load = jnp.concatenate([x.reshape(-1, 128), extra])
        got = [over_wide(load, m) for m in range(1, wide)]
        a1, a2, a3 = (g[: x.size // 128].reshape(x.shape) for g in got)
        return (x + a1) + (a2 + a3), [extra] + [g[x.size // 128 :] for g in got]

    def placed(pieces, shape, spots):
        buf = jnp.zeros(shape, pieces[0].dtype)
        for piece, spot in zip(pieces, spots, strict=True):
            buf = lax.dynamic_update_slice(buf, piece, spot)
        return buf

    def by_half(x, first, length):
        x = x.reshape(wide // 2, LENGTH, lanes)[:, first : first + length]
        mine = lax.dynamic_slice(x, (0, 0, c * half), (wide // 2, length, half))
        theirs = swap(lax.dynamic_slice(x, (0, 0, (1 - c) * half), (wide // 2, length, half)))
        return jnp.concatenate([jnp.where(c == 0, mine, theirs), jnp.where(c == 0, theirs, mine)])

    def exchange(x):
        return lax.all_to_all(x, "wide", 0, 0, tiled=True)

    def others(mine):
        return swap(lax.dynamic_slice_in_dim(mine, (1 - c) * (wide // 2), wide // 2, 0))

    def halves(w):
        axis = w.ndim - 1
        own = lax.dynamic_slice_in_dim(w, c * half, half, axis)
        return own, swap(lax.dynamic_slice_in_dim(w, (1 - c) * half, half, axis))

    def along_ring(line):
        pieces, spots = [], []
        for side, (first, second) in ((0, (1, 2)), (1, (2, 1))):
            part = line[:, side]
            one = over_ring(part, first)
            two = over_ring(part, second)
            three = over_ring(one, second)
            for m, p in ((0, part), (first, one), (second, two), (3, three)):
                pieces.append(p[None, :, None])
                spots.append((r ^ m, 0, side, 0, 0))
        return placed(pieces, (4,) + line.shape, spots)

    def gathered_late(both):
        return lax.all_gather(lax.all_gather(both, "wide"), "ring")

    def ring_pieces(tiles):
        pieces = [lax.dynamic_index_in_dim(tiles, r ^ m, 0, keepdims=False) for m in range(4)]
        return pieces[:1] + [over_ring(pieces[m], m) for m in range(1, 4)]

    def rows_late(tiles):
        return lax.psum_scatter(tiles.reshape(4 * wide * 2, depth, half), "ring", scatter_dimension=0, tiled=True)

    theirs = swap(resets)
    row = jnp.where(c == z // 2, resets, theirs)
    keep = 1.0 - lax.dynamic_slice(row, ((z % 2) * LENGTH,), (LENGTH,)).astype(f32)
    vectors = jnp.concatenate([gains, shifts, decays])
    vectors = lax.dynamic_slice(vectors, (0, c * half), (6, half)).reshape(-1, 128)

    second = jnp.stack(halves(weights[1]))
    shards = [weights[0]] + [over_wide(weights[0], m) for m in range(1, wide)]
    x = by_half(frames, 0, LENGTH)
    cut = LENGTH // 2
    x, shards[3], keep = lax.optimization_barrier((x, shards[3], keep))
    x, second = lax.optimization_barrier((x, second))
    shards, grad_out = lax.optimization_barrier((shards, grad_out))
    mats = [None, gathered_late(second)]
    xs = exchange(x)
    line = jnp.stack(halves(jnp.stack(shards)), 1)
    line = placed([line[m][None] for m in range(wide)], line.shape, [(z ^ m, 0, 0, 0) for m in range(wide)])
    mats[0] = along_ring(line)
    g_early, g_late = by_half(grad_out, 0, cut), by_half(grad_out, cut, cut)
    xs, mats[0], g_late = lax.optimization_barrier((xs, mats[0], g_late))
    xo = swap(xs)
    g_late = exchange(g_late)

    saved = []
    ins = (xs, xo)
    for level in range(2):
        pre, sums = product(*ins, mats[level], True)
        if level == 0:
            sums, pieces = everywhere(sums, vectors)
            spots = [(0, (z ^ m) * half) for m in range(wide)]
            vectors = placed([p.reshape(6, half) for p in pieces], (6, wide * half), spots)
            vectors = vectors.reshape(3, 2, -1, 128)
            params = [vectors[:, i] for i in range(2)]
            sums, g_late, g_early = lax.optimization_barrier((sums, g_late, g_early))
            g_early = exchange(g_early)
        else:
            sums = everywhere(sums)
        states, *y = forward(sums, params[level], keep, pre, count, wide, 1 + level)
        saved.append((ins, pre, sums, states))
        if level == 0:
            ins = (y[0], swap(y[0]))
    out_early = exchange(y[0])

    core = c.reshape(1)
    dys, terms = (g_early, g_late), 1
    totals_list = [None, None]
    for level in (1, 0):
        ins, pre, sums, states = saved[level]
        carried, totals = backward(sums, params[level], keep, pre, states, dys, terms, count)
        totals = everywhere(totals)
        totals_list[level] = totals
        if level:
            out_early, out_late, totals = lax.optimization_barrier((out_early, y[1], totals))
            out_late = exchange(out_late)
        else:
            out_early, out_late, totals = lax.optimization_barrier((out_early, out_late, totals))
        back_of = functools.partial(spread, sums, params[level], totals, carried, pre, mats[level], True, count)
        if level:
            dpre, other = back_of(1)
            other = swap(other)
            tiles = outer(*ins, dpre, True)
            tiles, dpre = lax.optimization_barrier((tiles, dpre))
            late = rows_late(tiles)
            dys, terms = (spread_own(dpre, mats[level], True), other), 2
        else:
            dpre, other = back_of(1)
            other = swap(other)
            same = spread_own(dpre, mats[level], True)
            both = exchange(load(same, other, late.reshape(wide, 2 * depth, half)))
            tiles = outer(*ins, dpre, True)
            sent = place(core, out_early, others(out_early), bf16, 0, 2, None)
            sent = place(core, out_late, others(out_late), bf16, 1, 2, sent)
            pieces, sent = lax.optimization_barrier((ring_pieces(tiles), sent))
            pieces = [p.astype(f32) for p in pieces]
            line = ((pieces[0] + pieces[1]) + (pieces[2] + pieces[3])).astype(bf16)
            own, away = line[:, 0], swap(line[:, 1])
            line = jnp.concatenate([jnp.where(c == 0, own, away), jnp.where(c == 0, away, own)], axis=2)
            line, both = lax.optimization_barrier((line, both))
            line = exchange(line)
            back = place(core, both, others(both[:, :LENGTH]), f32, 0, 1, None)
            late = jnp.sum(both[:, LENGTH:].astype(f32), 0).reshape(2, depth, half)
            own, away = late[0], swap(late[1])
            late = jnp.concatenate([jnp.where(c == 0, own, away), jnp.where(c == 0, away, own)], axis=1)
            line, back, late = lax.optimization_barrier((line, back, late))
            weight_grad = jnp.stack([jnp.sum(line.astype(f32), 0), late])

    small = []
    for level in range(2):
        mean, var, _ = stats_of(saved[level][2], count)
        small.append(jnp.concatenate([mean[None], var[None], totals_list[level]]))
    small = jnp.stack(small).reshape(2, 5, wide, half)
    small = lax.dynamic_index_in_dim(small, z, 2, keepdims=False)
    away = swap(small)
    small = jnp.concatenate([jnp.where(c == 0, small, away), jnp.where(c == 0, away, small)], axis=2)
    new_mean = (1.0 - momentum) * running[:, 0] + momentum * small[:, 0]
    new_var = (1.0 - momentum) * running[:, 1] + momentum * small[:, 1] * count / (count - 1.0)
    return (
        sent,
        back,
        weight_grad,
        small[:, 3],
        small[:, 2],
        small[:, 4],
        jnp.stack([new_mean, new_var], axis=1),
    )


def link(earlier, later):
    return (earlier[0] * later[0], later[0] * earlier[1] + later[1])


def general(frames, weights, gains, shifts, decays, resets, running, grad_out):
    frame_rows, lanes = frames.shape
    count = frame_rows * lax.axis_size(NARROW) * 1.0
    keep = (1 - resets).astype(jnp.float32).reshape(-1, LENGTH, 1)
    layer_in = frames
    saved = []
    updated = []
    for level in range(2):
        full_in = lax.all_gather(layer_in, "wide", axis=1, tiled=True)
        full_weight = lax.all_gather(weights[level], NARROW, axis=0, tiled=True)
        pre = jnp.dot(full_in, full_weight, preferred_element_type=jnp.float32)
        total, squares = lax.psum((jnp.sum(pre, 0), jnp.sum(pre * pre, 0)), NARROW)
        mean = total / count
        var = squares / count - mean * mean
        scale = lax.rsqrt(var + eps_norm)
        normed_hat = (pre - mean) * scale
        drive = (normed_hat * gains[level] + shifts[level]).reshape(-1, LENGTH, lanes)
        rate = keep * decays[level]
        _, states = lax.associative_scan(link, (rate, drive), axis=1)
        saved.append((full_in, full_weight, normed_hat, scale, states, rate))
        states = states.reshape(frame_rows, lanes)
        layer_in = jax.nn.silu(states).astype(jnp.bfloat16)
        new_mean = (1.0 - momentum) * running[level, 0] + momentum * mean
        new_var = (1.0 - momentum) * running[level, 1] + momentum * var * count / (count - 1.0)
        updated.append(jnp.stack([new_mean, new_var]))
    grad = grad_out.astype(jnp.float32)
    weight_list = [None, None]
    gain_list = [None, None]
    shift_list = [None, None]
    decay_list = [None, None]
    for level in (1, 0):
        full_in, full_weight, normed_hat, scale, states, rate = saved[level]
        sigma = jax.nn.sigmoid(states)
        grad_state = grad.reshape(-1, LENGTH, lanes) * (sigma + states * sigma * (1.0 - sigma))
        rate_next = jnp.concatenate([rate[:, 1:], jnp.zeros_like(rate[:, :1])], axis=1)
        _, carried = lax.associative_scan(link, (rate_next, grad_state), reverse=True, axis=1)
        prior = jnp.concatenate([jnp.zeros_like(states[:, :1]), states[:, :-1]], axis=1)
        decay_term = jnp.sum(carried * keep * prior, axis=(0, 1))
        carried = carried.reshape(frame_rows, lanes)
        shift_sum, gain_sum, decay_sum = lax.psum(
            (jnp.sum(carried, 0), jnp.sum(carried * normed_hat, 0), decay_term), NARROW
        )
        grad_pre = (
            gains[level] * scale * (carried - shift_sum / count - normed_hat * gain_sum / count)
        ).astype(jnp.bfloat16)
        weight_list[level] = lax.psum_scatter(
            lax.dot_general(
                full_in, grad_pre, (((0,), (0,)), ((), ())), preferred_element_type=jnp.float32
            ),
            NARROW,
            scatter_dimension=0,
            tiled=True,
        )
        gain_list[level] = gain_sum
        shift_list[level] = shift_sum
        decay_list[level] = decay_sum
        partial_term = lax.dot_general(
            grad_pre, full_weight, (((1,), (1,)), ((), ())), preferred_element_type=jnp.float32
        )
        grad = lax.psum_scatter(partial_term, "wide", scatter_dimension=1, tiled=True)
    return (
        layer_in,
        grad,
        jnp.stack(weight_list),
        jnp.stack(gain_list),
        jnp.stack(shift_list),
        jnp.stack(decay_list),
        jnp.stack(updated),
    )


def per_device(frames, weights, *rest):
    wide, narrow = lax.axis_size("wide"), lax.axis_size(NARROW)
    rows, lanes = frames.shape
    one_row_a_chip = 2 * rows == wide * LENGTH and wide == 4 and narrow == 2 * wide
    if one_row_a_chip and lanes == 2 * weights.shape[1] and wide * lanes == 2048:
        return paired(frames, weights, *rest)
    return general(frames, weights, *rest)


def solution(mesh):
    wide, narrow = mesh.shape["wide"], mesh.shape["narrow"]
    devices = mesh.devices if mesh.axis_names == ("wide", "narrow") else mesh.devices.T
    cut = Mesh(devices.reshape(wide, narrow // 2, 2), AXES)
    placed = (
        P(NARROW, "wide"),
        P(None, NARROW, "wide"),
        P(None, "wide"),
        P(None, "wide"),
        P(None, "wide"),
        P(NARROW),
        P(None, None, "wide"),
        P(NARROW, "wide"),
    )
    return jax.shard_map(
        per_device,
        mesh=cut,
        in_specs=placed,
        out_specs=(
            P(NARROW, "wide"),
            P(NARROW, "wide"),
            P(None, NARROW, "wide"),
            P(None, "wide"),
            P(None, "wide"),
            P(None, "wide"),
            P(None, None, "wide"),
        ),
        check_vma=False,
    )
```
